128 devices in a mesh: row: 16 (over y, x_hi, core), col: 8 (over x_lo, z).
Axes of the slice: x: 4 (x_hi: 2, x_lo: 2; x = x_hi * 2 + x_lo), y: 4, z: 4, core: 2. Of those that a mesh axis runs over, the one named last changes fastest.
Arguments:
- pair: bfloat16 [448, 448, 128], P('row', 'col'), may hold values from -6 to 6
- cotangent: bfloat16 [448, 448, 128], P('row', 'col'), may hold values from -6 to 6
- w_a_proj: bfloat16 [128, 128], replicated, may hold values from -0.5 to 0.5
- w_a_gate: bfloat16 [128, 128], replicated, may hold values from -0.5 to 0.5
- w_b_proj: bfloat16 [128, 128], replicated, may hold values from -0.5 to 0.5
- w_b_gate: bfloat16 [128, 128], replicated, may hold values from -0.5 to 0.5
- w_gate: bfloat16 [128, 128], replicated, may hold values from -0.5 to 0.5
- w_out: bfloat16 [128, 128], replicated, may hold values from -0.5 to 0.5
- in_gain: float32 [128], replicated, may hold values from 0.5 to 1.5
- in_bias: float32 [128], replicated, may hold values from -1.5 to 1.5
- mid_gain: float32 [128], replicated, may hold values from 0.1 to 1.9
- mid_bias: float32 [128], replicated, may hold values from -1.5 to 1.5
- drop_bits: int32 [448, 128], P('row'), may hold values 0 or 1
- tok_mask: int32 [448], replicated, may hold values from 0 to 1, as said below
Outputs:
- result: bfloat16 [448, 448, 128], P('row', 'col')
- pair_grad: bfloat16 [448, 448, 128], P('row', 'col')
- a_proj_grad: float32 [128, 128], replicated
- a_gate_grad: float32 [128, 128], replicated
- b_proj_grad: float32 [128, 128], replicated
- b_gate_grad: float32 [128, 128], replicated
- gate_grad: float32 [128, 128], replicated
- out_grad: float32 [128, 128], replicated
- in_gain_grad: float32 [128], replicated
- in_bias_grad: float32 [128], replicated
- mid_gain_grad: float32 [128], replicated
- mid_bias_grad: float32 [128], replicated
The draws below stay inside these ranges and needn't reach their ends.
Inputs may be any that keep to these rules, and one draw needn't show every extreme that they name: `tok_mask`: 1 on the live tokens, which form a prefix of 224 or more tokens, 0 on the rest; at least one token is padding.
All inputs are finite; a program needn't handle non-finite values. No bound on the sum of `drop_bits` on one device may be relied on, other than what follows from the above.
Results may differ from the reference program's by a relative error of at most 0.012.
Values may be sent and summed in bfloat16 or wider, within the bound.
A program may use at most 128 MiB of HBM per device.

```python
import jax
import jax.numpy as jnp
from jax import lax

C = 128
H = 128
NTOK = 448


def draw_tok_mask(key, part):
    key = jax.random.fold_in(key, 7)
    live_count = jax.random.randint(key, (), NTOK // 2, NTOK)
    return (jnp.arange(NTOK) < live_count).astype(jnp.int32)


def place_ends(entries, stream_key, low, top_value):
    dims = entries.shape
    index_at = [jax.random.randint(jax.random.fold_in(stream_key, axis), (), 0, dims[axis]) for axis in range(len(dims))]
    entries = entries.at[tuple(index_at)].set(low)
    longest = dims.index(max(dims))
    index_at[longest] = (index_at[longest] + 1) % dims[longest]
    return entries.at[tuple(index_at)].set(top_value)


def steps_of(stream_key, extent, cuts, smallest, largest):
    loudness, own = 1.0, jax.random.fold_in(stream_key, 6)
    for position, shards_of in cuts:
        draws = jnp.exp(jax.random.uniform(jax.random.fold_in(own, position), (shards_of,), jnp.float32, smallest / len(cuts), largest / len(cuts)))
        loudness = loudness * jnp.repeat(draws, extent[position] // shards_of).reshape([-1 if axis == position else 1 for axis in range(len(extent))])
    return loudness


def noise(rng, shape, spread, reach, pieces=(), kind=jnp.bfloat16):
    level = steps_of(rng, shape, pieces, -0.22, 0.18) if pieces else 1.0
    values = jax.random.normal(rng, shape, jnp.float32) * spread * level
    return jnp.minimum(jnp.maximum(values, -reach), reach).astype(kind)


def setup_inputs(seed: int = 0) -> dict:
    arg_keys = jax.random.split(jax.random.key(seed), 15)
    pair = noise(arg_keys[0], (NTOK, NTOK, C), 1.0, 6.0, ((0, 16), (1, 8)))
    cotangent = noise(arg_keys[1], (NTOK, NTOK, C), 1.0, 6.0, ((0, 16), (1, 8)))
    w_a_proj = noise(arg_keys[2], (C, H), C ** -0.5, 0.5)
    w_a_gate = noise(arg_keys[3], (C, H), C ** -0.5, 0.5)
    w_b_proj = noise(arg_keys[4], (C, H), C ** -0.5, 0.5)
    w_b_gate = noise(arg_keys[5], (C, H), C ** -0.5, 0.5)
    w_gate = noise(arg_keys[6], (C, C), C ** -0.5, 0.5)
    w_out = noise(arg_keys[7], (H, C), H ** -0.5, 0.5)
    in_gain = jnp.clip(1.0 + 0.1 * jax.random.normal(arg_keys[8], (C,), jnp.float32), 0.5, 1.5)
    in_bias = noise(arg_keys[9], (C,), 0.3, 1.5, (), jnp.float32)
    mid_gain = jnp.clip(1.0 + 0.18 * jax.random.normal(arg_keys[10], (H,), jnp.float32), 0.1, 1.9)
    mid_bias = noise(arg_keys[11], (H,), 0.3, 1.5, (), jnp.float32)
    drop_bits = place_ends((jax.random.randint(arg_keys[12], (NTOK, C), 0, 4) < 3).astype(jnp.int32), jax.random.fold_in(arg_keys[12], 1), 0, 1)
    tok_mask = draw_tok_mask(jax.random.fold_in(arg_keys[14], 71), 0)
    return {"pair": pair, "cotangent": cotangent, "w_a_proj": w_a_proj, "w_a_gate": w_a_gate, "w_b_proj": w_b_proj, "w_b_gate": w_b_gate, "w_gate": w_gate, "w_out": w_out, "in_gain": in_gain, "in_bias": in_bias, "mid_gain": mid_gain, "mid_bias": mid_bias, "drop_bits": drop_bits, "tok_mask": tok_mask}


LN_EPS = 1e-05
KEEP_RATE = 0.75

def layer_norm(values, gain, bias):
    average = lax.optimization_barrier(jnp.mean(values, axis=-1, keepdims=True))
    centered = values - average
    variance = lax.optimization_barrier(jnp.mean(centered * centered, axis=-1, keepdims=True))
    return centered * lax.rsqrt(variance + LN_EPS) * gain + bias

def project_rows(values, weight):
    flat = values.reshape(-1, values.shape[-1])
    out_flat = jnp.dot(flat, weight, preferred_element_type=jnp.float32)
    return out_flat.reshape(values.shape[:-1] + (weight.shape[1],))

def back_project(cotan, weight):
    flat = cotan.reshape(-1, cotan.shape[-1])
    out_flat = lax.dot_general(flat, weight, (((1,), (1,)), ((), ())), preferred_element_type=jnp.float32)
    return out_flat.reshape(cotan.shape[:-1] + (weight.shape[0],))

def weight_grad(values, cotan):
    left = values.reshape(-1, values.shape[-1])
    right = cotan.reshape(-1, cotan.shape[-1])
    return lax.dot_general(left, right, (((0,), (0,)), ((), ())), preferred_element_type=jnp.float32)

def front_forward(pair, in_gain, in_bias, w_a_proj, w_a_gate, w_b_proj, w_b_gate, row_mask, col_mask):
    normed = layer_norm(pair.astype(jnp.float32), in_gain, in_bias).astype(jnp.bfloat16)
    pair_mask = (row_mask[:, None] * col_mask[None, :]).astype(jnp.float32)[:, :, None]
    a_proj = project_rows(normed, w_a_proj)
    a_gate = project_rows(normed, w_a_gate)
    b_proj = project_rows(normed, w_b_proj)
    b_gate = project_rows(normed, w_b_gate)
    a_values = (jax.nn.sigmoid(a_gate) * a_proj * pair_mask).astype(jnp.bfloat16)
    b_values = (jax.nn.sigmoid(b_gate) * b_proj * pair_mask).astype(jnp.bfloat16)
    return (normed, a_values, b_values, (a_proj, a_gate, b_proj, b_gate, pair_mask))

def gate_grads(cotan, projected, gate_logit, pair_mask):
    masked = cotan.astype(jnp.float32) * pair_mask
    squash = jax.nn.sigmoid(gate_logit)
    d_proj = (masked * squash).astype(jnp.bfloat16)
    d_gate = (masked * projected * squash * (1.0 - squash)).astype(jnp.bfloat16)
    return (d_proj, d_gate)

def front_backward(pair, normed, saved, grad_a, grad_b, grad_normed_tail, in_gain, in_bias, w_a_proj, w_a_gate, w_b_proj, w_b_gate):
    a_proj, a_gate, b_proj, b_gate, pair_mask = saved
    d_a_proj, d_a_gate = gate_grads(grad_a, a_proj, a_gate, pair_mask)
    d_b_proj, d_b_gate = gate_grads(grad_b, b_proj, b_gate, pair_mask)
    grad_normed = grad_normed_tail + back_project(d_a_proj, w_a_proj) + back_project(d_a_gate, w_a_gate)
    grad_normed = grad_normed + back_project(d_b_proj, w_b_proj) + back_project(d_b_gate, w_b_gate)
    outputs, norm_vjp = jax.vjp(layer_norm, pair.astype(jnp.float32), in_gain, in_bias)
    d_pair, d_gain, d_bias = norm_vjp(grad_normed)
    weights = (weight_grad(normed, d_a_proj), weight_grad(normed, d_a_gate), weight_grad(normed, d_b_proj), weight_grad(normed, d_b_gate))
    return (d_pair, weights, d_gain, d_bias)

def tail_forward(pair, product, normed, mid_gain, mid_bias, w_gate, w_out, drop_bits):
    mixed = layer_norm(product, mid_gain, mid_bias).astype(jnp.bfloat16)
    lifted = project_rows(mixed, w_out)
    squash = jax.nn.sigmoid(project_rows(normed, w_gate))
    keep_scale = (drop_bits.astype(jnp.float32) / KEEP_RATE)[:, None, :]
    result = (pair.astype(jnp.float32) + keep_scale * lifted * squash).astype(jnp.bfloat16)
    return (result, (mixed, lifted, squash, keep_scale))

def tail_backward(cotangent, product, normed, saved, mid_gain, mid_bias, w_gate, w_out):
    mixed, lifted, squash, keep_scale = saved
    upstream = cotangent.astype(jnp.float32)
    d_update = upstream * keep_scale
    d_lifted = (d_update * squash).astype(jnp.bfloat16)
    d_logit = (d_update * lifted * squash * (1.0 - squash)).astype(jnp.bfloat16)
    grad_mixed = back_project(d_lifted, w_out)
    grad_normed = back_project(d_logit, w_gate)
    outputs, norm_vjp = jax.vjp(layer_norm, product, mid_gain, mid_bias)
    d_product, d_gain, d_bias = norm_vjp(grad_mixed)
    weights = (weight_grad(normed, d_logit), weight_grad(mixed, d_lifted))
    return (upstream, d_product, grad_normed, weights, d_gain, d_bias)

def reference(pair, cotangent, w_a_proj, w_a_gate, w_b_proj, w_b_gate, w_gate, w_out, in_gain, in_bias, mid_gain, mid_bias, drop_bits, tok_mask):
    normed, a_values, b_values, front_saved = front_forward(pair, in_gain, in_bias, w_a_proj, w_a_gate, w_b_proj, w_b_gate, tok_mask, tok_mask)
    a_float = lax.optimization_barrier(a_values).astype(jnp.float32)
    b_float = lax.optimization_barrier(b_values).astype(jnp.float32)
    product = jnp.einsum('kih,kjh->ijh', a_float, b_float)
    result, tail_saved = tail_forward(pair, product, normed, mid_gain, mid_bias, w_gate, w_out, drop_bits)
    upstream, d_product, grad_normed, tail_weights, d_mid_gain, d_mid_bias = tail_backward(cotangent, product, normed, tail_saved, mid_gain, mid_bias, w_gate, w_out)
    d_round = lax.optimization_barrier(d_product.astype(jnp.bfloat16)).astype(jnp.float32)
    grad_a = jnp.einsum('kjh,ijh->kih', b_float, d_round).astype(jnp.bfloat16)
    grad_b = jnp.einsum('kih,ijh->kjh', a_float, d_round).astype(jnp.bfloat16)
    d_pair, front_weights, d_in_gain, d_in_bias = front_backward(pair, normed, front_saved, grad_a, grad_b, grad_normed, in_gain, in_bias, w_a_proj, w_a_gate, w_b_proj, w_b_gate)
    pair_grad = (upstream + d_pair).astype(jnp.bfloat16)
    factor = 1.0 / NTOK
    return (result, pair_grad, front_weights[0] * factor, front_weights[1] * factor, front_weights[2] * factor, front_weights[3] * factor, tail_weights[0] * factor, tail_weights[1] * factor, d_in_gain * factor, d_in_bias * factor, d_mid_gain * factor, d_mid_bias * factor)
```

```python
import functools

import jax
import jax.numpy as jnp
from jax import lax
from jax.experimental import pallas as pl
from jax.experimental.pallas import tpu as pltpu
from jax.sharding import PartitionSpec as P

LN_EPS = 1e-05
KEEP_RATE = 0.75
ROWS, COLS = 16, 8
DEVICES = ROWS * COLS
TR, TC = 28, 56
TOKENS = 448


def exchange_kernel(spread, x_ref, o_ref, send_sem, recv_sem):
    me = lax.axis_index("row") * COLS + lax.axis_index("col")
    barrier = pltpu.get_barrier_semaphore()

    def greet(step, carry):
        peer = lax.rem(me + step, DEVICES)
        pl.semaphore_signal(
            barrier,
            inc=1,
            device_id=(peer // COLS, lax.rem(peer, COLS)),
            device_id_type=pl.DeviceIdType.MESH,
        )
        return carry

    lax.fori_loop(1, DEVICES, greet, 0)
    pl.semaphore_wait(barrier, DEVICES - 1)

    def send(step, carry):
        peer = lax.rem(me + step, DEVICES)
        pltpu.make_async_remote_copy(
            src_ref=x_ref.at[0 if spread else peer],
            dst_ref=o_ref.at[me],
            send_sem=send_sem,
            recv_sem=recv_sem,
            device_id=(peer // COLS, lax.rem(peer, COLS)),
            device_id_type=pl.DeviceIdType.MESH,
        ).start()
        return carry

    lax.fori_loop(1, DEVICES, send, 0)
    o_ref[me] = x_ref[0 if spread else me]
    others = o_ref.at[pl.ds(0, DEVICES - 1)]
    pltpu.make_async_copy(others, others, recv_sem).wait()
    pltpu.make_async_copy(others, others, send_sem).wait()


def exchange(blocks, collective, spread=False):
    shape = (DEVICES,) + blocks.shape[1:]
    return pl.pallas_call(
        functools.partial(exchange_kernel, spread),
        out_shape=jax.ShapeDtypeStruct(shape, blocks.dtype),
        in_specs=[pl.BlockSpec(memory_space=pltpu.VMEM)],
        out_specs=pl.BlockSpec(memory_space=pltpu.VMEM),
        scratch_shapes=[pltpu.SemaphoreType.DMA, pltpu.SemaphoreType.DMA],
        compiler_params=pltpu.CompilerParams(
            collective_id=collective, has_side_effects=True, vmem_limit_bytes=16 * 2**20
        ),
    )(blocks)


def pack(tile):
    padded = jnp.pad(tile, ((0, 4), (0, 8), (0, 0))).reshape(2, 16, 64, 128)
    return padded.transpose(3, 1, 0, 2).reshape(128, 16, 128)


def unpack(blocks):
    spread = blocks.reshape(128, 16, 2, 64).transpose(2, 1, 3, 0).reshape(32, 64, 128)
    return spread[:TR, :TC]


def assemble(blocks):
    spread = blocks.reshape(ROWS, COLS, 16, 2, 64).transpose(0, 3, 2, 1, 4)
    return spread.reshape(ROWS, 32, COLS, 64)[:, :TR, :, :TC].reshape(TOKENS, TOKENS)


def split(matrix):
    padded = jnp.pad(
        matrix.reshape(ROWS, TR, COLS, TC), ((0, 0), (0, 4), (0, 0), (0, 8))
    )
    spread = padded.reshape(ROWS, 2, 16, COLS, 64).transpose(0, 3, 2, 1, 4)
    return spread.reshape(DEVICES, 16, 128)


def layer_norm(values, gain, bias):
    average = jnp.mean(values, axis=-1, keepdims=True)
    centered = values - average
    variance = jnp.mean(centered * centered, axis=-1, keepdims=True)
    return centered * lax.rsqrt(variance + LN_EPS) * gain + bias


def project_rows(values, weight):
    return lax.dot_general(
        values, weight, (((2,), (0,)), ((), ())), preferred_element_type=jnp.float32
    )


def back_project(cotan, weight):
    return lax.dot_general(
        cotan, weight, (((2,), (1,)), ((), ())), preferred_element_type=jnp.float32
    )


def weight_grad(values, cotan):
    return lax.dot_general(
        values, cotan, (((0, 1), (0, 1)), ((), ())), preferred_element_type=jnp.float32
    )


def gate_grads(cotan, projected, gate_logit, pair_mask):
    masked = cotan.astype(jnp.float32) * pair_mask
    squash = jax.nn.sigmoid(gate_logit)
    d_proj = (masked * squash).astype(jnp.bfloat16)
    d_gate = (masked * projected * squash * (1.0 - squash)).astype(jnp.bfloat16)
    return (d_proj, d_gate)


def body(
    pair,
    cotangent,
    w_a_proj,
    w_a_gate,
    w_b_proj,
    w_b_gate,
    w_gate,
    w_out,
    in_gain,
    in_bias,
    mid_gain,
    mid_bias,
    drop_bits,
    tok_mask,
):
    bf16 = jnp.bfloat16
    row_mask = lax.dynamic_slice_in_dim(tok_mask, lax.axis_index("row") * TR, TR)
    col_mask = lax.dynamic_slice_in_dim(tok_mask, lax.axis_index("col") * TC, TC)
    pair_mask = (row_mask[:, None] * col_mask[None, :]).astype(jnp.float32)[:, :, None]
    wide = pair.astype(jnp.float32)
    normed = layer_norm(wide, in_gain, in_bias).astype(bf16)
    a_proj = project_rows(normed, w_a_proj)
    a_gate = project_rows(normed, w_a_gate)
    b_proj = project_rows(normed, w_b_proj)
    b_gate = project_rows(normed, w_b_gate)
    a_values = (jax.nn.sigmoid(a_gate) * a_proj * pair_mask).astype(bf16)
    b_values = (jax.nn.sigmoid(b_gate) * b_proj * pair_mask).astype(bf16)
    got = exchange(jnp.concatenate([pack(a_values), pack(b_values)], axis=1), 0)
    a_full, b_full = assemble(got[:, :16]), assemble(got[:, 16:])
    product = lax.dot_general(
        a_full, b_full, (((0,), (0,)), ((), ())), preferred_element_type=jnp.float32
    ).astype(bf16)
    product = unpack(exchange(split(product), 1)).astype(jnp.float32)

    mixed = layer_norm(product, mid_gain, mid_bias).astype(bf16)
    lifted = project_rows(mixed, w_out)
    squash = jax.nn.sigmoid(project_rows(normed, w_gate))
    keep_scale = (drop_bits.astype(jnp.float32) / KEEP_RATE)[:, None, :]
    result = (wide + keep_scale * lifted * squash).astype(bf16)
    upstream = cotangent.astype(jnp.float32)
    d_update = upstream * keep_scale
    d_lifted = (d_update * squash).astype(bf16)
    d_logit = (d_update * lifted * squash * (1.0 - squash)).astype(bf16)
    grad_mixed = back_project(d_lifted, w_out)
    grad_normed = back_project(d_logit, w_gate)
    _, norm_vjp = jax.vjp(layer_norm, product, mid_gain, mid_bias)
    d_product, d_mid_gain, d_mid_bias = norm_vjp(grad_mixed)
    d_full = assemble(exchange(pack(d_product.astype(bf16)), 1))
    grad_a = lax.dot_general(
        b_full, d_full, (((1,), (1,)), ((), ())), preferred_element_type=jnp.float32
    ).astype(bf16)
    grad_b = lax.dot_general(
        a_full, d_full, (((1,), (0,)), ((), ())), preferred_element_type=jnp.float32
    ).astype(bf16)
    got = exchange(jnp.concatenate([split(grad_a), split(grad_b)], axis=1), 0)
    grad_a, grad_b = unpack(got[:, :16]), unpack(got[:, 16:])

    d_a_proj, d_a_gate = gate_grads(grad_a, a_proj, a_gate, pair_mask)
    d_b_proj, d_b_gate = gate_grads(grad_b, b_proj, b_gate, pair_mask)
    grad_normed = grad_normed + back_project(d_a_proj, w_a_proj) + back_project(d_a_gate, w_a_gate)
    grad_normed = grad_normed + back_project(d_b_proj, w_b_proj) + back_project(d_b_gate, w_b_gate)
    _, norm_vjp = jax.vjp(layer_norm, wide, in_gain, in_bias)
    d_pair, d_gain, d_bias = norm_vjp(grad_normed)
    pair_grad = (upstream + d_pair).astype(bf16)

    vectors = jnp.zeros((2, 128, 128), jnp.float32)
    vectors = vectors.at[0, :4].set(jnp.stack([d_gain, d_bias, d_mid_gain, d_mid_bias]))
    sums = jnp.stack(
        [
            weight_grad(normed, d_a_proj),
            weight_grad(normed, d_a_gate),
            weight_grad(normed, d_b_proj),
            weight_grad(normed, d_b_gate),
            weight_grad(normed, d_logit),
            weight_grad(mixed, d_lifted),
            vectors[0],
            vectors[1],
        ],
        axis=1,
    )
    share = jnp.sum(exchange(sums, 2), axis=0, keepdims=True) * (1.0 / TOKENS)
    summed = exchange(share, 3, spread=True).transpose(1, 0, 2)
    return (result, pair_grad) + tuple(summed[n] for n in range(6)) + tuple(
        summed[6, n] for n in range(4)
    )


def solution(mesh):
    tiles = P("row", "col", None)
    return jax.shard_map(
        body,
        mesh=mesh,
        in_specs=(tiles, tiles) + (P(),) * 10 + (P("row", None), P()),
        out_specs=(tiles, tiles) + (P(),) * 10,
        check_vma=False,
    )
```

```python
import jax
import jax.numpy as jnp
from jax import lax
from jax.experimental import pallas as pl
from jax.experimental.pallas import tpu as pltpu
from jax.sharding import PartitionSpec as P

LN_EPS = 1e-05
KEEP_RATE = 0.75
ROWS, COLS = 16, 8
DEVICES = ROWS * COLS
TR, TC = 28, 56
TOKENS = 448
WIDE = 256
STEPS = 8
CELLS = WIDE * STEPS
SIDE = 512
PART = 16
SPAN = (DEVICES - 1) * PART
ORDER = 37
BF16 = jnp.bfloat16
F32 = jnp.float32


def dot(left, right):
    return jnp.dot(left, right, preferred_element_type=F32)


def dot_nt(left, right):
    return lax.dot_general(left, right, (((1,), (1,)), ((), ())), preferred_element_type=F32)


def dot_tn(left, right):
    return lax.dot_general(left, right, (((0,), (0,)), ((), ())), preferred_element_type=F32)


def mean0(values):
    return jnp.mean(values, axis=0, keepdims=True)


def swap_halves(first, second):
    low = lax.broadcasted_iota(jnp.int32, first.shape, 1) < 64
    turned_first = pltpu.roll(first, 64, 1)
    turned_second = pltpu.roll(second, 64, 1)
    return jnp.where(low, first, turned_second), jnp.where(low, turned_first, second)


def kernel(
    pair,
    cot,
    w_a_proj,
    w_a_gate,
    w_b_proj,
    w_b_gate,
    w_gate,
    w_out,
    in_gain,
    in_bias,
    mid_gain,
    mid_bias,
    drop,
    tok,
    result,
    pair_grad,
    sums,
    send_a,
    send_b,
    send_p,
    send_d,
    send_ga,
    send_gb,
    got_a,
    got_b,
    got_p,
    got_d,
    got_ga,
    got_gb,
    left,
    right,
    turn,
    square,
    flat_a,
    flat_b,
    eye,
    w_in_t,
    w_out_t,
    columns,
    drop_wide,
    normed,
    hat,
    scale,
    keep_a,
    slope_a,
    keep_b,
    slope_b,
    pair_t,
    cot_t,
    lift_keep,
    logit_keep,
    d_lifted,
    grad_mixed,
    mid_hat,
    mixed,
    d_logit,
    d_front,
    tail_normed,
    totals,
    sums_send,
    sums_got,
    share,
    send_sem,
    recv_sem,
):
    row, col = lax.axis_index("row"), lax.axis_index("col")
    me = row * COLS + col
    barrier = pltpu.get_barrier_semaphore()

    def place(peer):
        return (peer // COLS, lax.rem(peer, COLS))

    def greet(step, carry):
        pl.semaphore_signal(
            barrier,
            inc=1,
            device_id=place(lax.rem(me + step, DEVICES)),
            device_id_type=pl.DeviceIdType.MESH,
        )
        return carry

    lax.fori_loop(1, DEVICES, greet, 0)

    def send(source, target, slot):
        mine = pl.ds(pl.multiple_of(me * PART, PART), PART)

        def start(step, carry):
            peer = lax.rem(me + step * ORDER, DEVICES)
            pltpu.make_async_remote_copy(
                src_ref=source.at[pl.ds(pl.multiple_of(peer * PART, PART), PART)],
                dst_ref=target.at[mine],
                send_sem=send_sem.at[slot],
                recv_sem=recv_sem.at[slot],
                device_id=place(peer),
                device_id_type=pl.DeviceIdType.MESH,
            ).start()
            return carry

        lax.fori_loop(1, DEVICES, start, 0)
        target[mine] = source[mine]

    def arrived(target, slot, length=SPAN):
        others = target.at[pl.ds(0, length)]
        pltpu.make_async_copy(others, others, recv_sem.at[slot]).wait()

    def left_device(source, slot, length=SPAN):
        others = source.at[pl.ds(0, length)]
        pltpu.make_async_copy(others, others, send_sem.at[slot]).wait()

    def lanes(step):
        return pl.ds(pl.multiple_of(step * WIDE, WIDE), WIDE)

    def each(body):
        def run(step, carry):
            body(step, lanes(step))
            return carry

        lax.fori_loop(0, STEPS, run, 0)

    def scatter(flat, step, values):
        flat[pl.ds(2 * step, 128, stride=PART), :] = values[:, :128]
        flat[pl.ds(2 * step + 1, 128, stride=PART), :] = values[:, 128:]

    def gather(flat, step):
        return jnp.concatenate(
            [
                flat[pl.ds(2 * step, 128, stride=PART), :],
                flat[pl.ds(2 * step + 1, 128, stride=PART), :],
            ],
            axis=1,
        )

    def turned(ref, step):
        return jnp.concatenate(
            [dot_nt(eye[...], ref[2 * step]), dot_nt(eye[...], ref[2 * step + 1])], axis=1
        )

    def turn_back(ref, step, values):
        ref[2 * step] = dot_nt(eye[...], values[:, :128]).astype(BF16)
        ref[2 * step + 1] = dot_nt(eye[...], values[:, 128:]).astype(BF16)

    def assemble(blocks, matrix):
        def run(index, carry):
            base = pl.multiple_of(index * 128, 128)
            top = pl.multiple_of(index * 32, 32)
            for pick in range(4):
                one = blocks[pl.ds(base + 32 * pick, PART)].astype(F32)
                two = blocks[pl.ds(base + 32 * pick + PART, PART)].astype(F32)
                upper, lower = swap_halves(one, two)
                here = pl.ds(128 * pick, 128)
                matrix[pl.ds(top, PART), here] = upper.astype(BF16)
                matrix[pl.ds(top + PART, PART), here] = lower.astype(BF16)
            return carry

        lax.fori_loop(0, ROWS, run, 0)

    def split(matrix, blocks):
        def run(index, carry):
            base = pl.multiple_of(index * 128, 128)
            top = pl.multiple_of(index * 32, 32)
            for pick in range(4):
                here = pl.ds(128 * pick, 128)
                upper = matrix[pl.ds(top, PART), here]
                lower = matrix[pl.ds(top + PART, PART), here]
                one, two = swap_halves(upper, lower)
                blocks[pl.ds(base + 32 * pick, PART)] = one.astype(BF16)
                blocks[pl.ds(base + 32 * pick + PART, PART)] = two.astype(BF16)
            return carry

        lax.fori_loop(0, ROWS, run, 0)

    eye[...] = (
        lax.broadcasted_iota(jnp.int32, (128, 128), 0)
        == lax.broadcasted_iota(jnp.int32, (128, 128), 1)
    ).astype(BF16)
    for place_of, weight in enumerate((w_a_proj, w_a_gate, w_b_proj, w_b_gate, w_gate)):
        w_in_t[128 * place_of : 128 * place_of + 128] = dot_nt(eye[...], weight[...]).astype(BF16)
    w_out_t[...] = dot_nt(eye[...], w_out[...]).astype(BF16)
    for place_of, vector in enumerate((in_gain, in_bias, mid_gain, mid_bias)):
        column = jnp.broadcast_to(vector[...], (128, 128)).T
        columns[place_of] = jnp.concatenate([column, column], axis=1)
    drop_wide[...] = jnp.zeros_like(drop_wide)
    drop_wide[0:TR] = drop[...].astype(F32)
    live = jnp.sum(tok[...].astype(F32), axis=1, keepdims=True)

    def cell_mask(step):
        lane = lax.broadcasted_iota(jnp.int32, (1, WIDE), 1)
        tile_row = ((lane >> 6) & 1) * 16 + (lane >> 7) + 2 * step
        within = lane & 31
        tile_col = ((lane >> 5) & 1) * TR + within
        grid_row = (tile_row + row * TR).astype(F32)
        grid_col = (tile_col + col * TC).astype(F32)
        one = jnp.where(grid_row < live, 1.0, 0.0) * jnp.where(grid_col < live, 1.0, 0.0)
        return one * jnp.where(tile_row < TR, 1.0, 0.0) * jnp.where(within < TR, 1.0, 0.0)

    def front(step, here, weights, keep, slope, flat):
        logits = dot(w_in_t[weights], normed[:, here])
        squash = jax.nn.sigmoid(logits[128:])
        masked = squash * cell_mask(step)
        values = logits[:128] * masked
        keep[:, here] = masked
        slope[:, here] = values * (1.0 - squash)
        scatter(flat, step, values)

    def front_a(step, here):
        cells = turned(pair, step)
        pair_t[:, here] = cells
        centered = cells - mean0(cells)
        root = lax.rsqrt(mean0(centered * centered) + LN_EPS)
        rough = centered * root
        hat[:, here] = rough
        scale[:, here] = root
        normed[:, here] = (rough * columns[0] + columns[1]).astype(BF16)
        front(step, here, slice(0, 256), keep_a, slope_a, flat_a)

    each(front_a)
    send_a[...] = flat_a[...].astype(BF16)
    pl.semaphore_wait(barrier, DEVICES - 1)
    send(send_a, got_a, 0)
    each(lambda step, here: front(step, here, slice(256, 512), keep_b, slope_b, flat_b))
    send_b[...] = flat_b[...].astype(BF16)
    send(send_b, got_b, 1)

    def prepare(step, here):
        squash = jax.nn.sigmoid(dot(w_in_t[512:640], normed[:, here]))
        lane = lax.broadcasted_iota(jnp.int32, (32, WIDE), 1)
        chosen = ((lane >> 6) & 1) * 16 + (lane >> 7) + 2 * step
        pick = (lax.broadcasted_iota(jnp.int32, (32, WIDE), 0) == chosen).astype(BF16)
        bits = dot_tn(drop_wide[...].astype(BF16), pick)
        kept = bits * (1.0 / KEEP_RATE)
        upstream = turned(cot, step)
        cot_t[:, here] = upstream
        lift_keep[:, here] = kept * squash
        pulled = upstream * kept * squash
        logit_keep[:, here] = pulled * (1.0 - squash)
        lifted_back = pulled.astype(BF16)
        d_lifted[:, here] = lifted_back
        grad_mixed[:, here] = dot(w_out[...], lifted_back)

    each(prepare)
    arrived(got_a, 0)
    assemble(got_a, left)
    arrived(got_b, 1)
    assemble(got_b, right)
    square[...] = dot_tn(left[...], right[...])
    split(square, send_p)
    send(send_p, got_p, 2)

    arrived(got_p, 2)
    flat_a[...] = got_p[...].astype(F32)

    def tail_back(step, here):
        cells = gather(flat_a, step)
        centered = cells - mean0(cells)
        root = lax.rsqrt(mean0(centered * centered) + LN_EPS)
        rough = centered * root
        mid_hat[:, here] = rough
        pulled = grad_mixed[:, here] * columns[2]
        scatter(flat_b, step, root * (pulled - mean0(pulled) - rough * mean0(pulled * rough)))

    each(tail_back)
    send_d[...] = flat_b[...].astype(BF16)
    send(send_d, got_d, 3)

    totals[...] = jnp.zeros_like(totals)

    def total(which, values):
        totals[which] += values[:, :128] + values[:, 128:]

    def tail_front(step, here):
        rough = mid_hat[:, here]
        blended = (rough * columns[2] + columns[3]).astype(BF16)
        mixed[:, here] = blended
        lifted = dot(w_out_t[...], blended)
        turn_back(result, step, (pair_t[:, here] + lift_keep[:, here] * lifted).astype(BF16))
        logit = (logit_keep[:, here] * lifted).astype(BF16)
        d_logit[:, here] = logit
        tail_normed[:, here] = dot(w_gate[...], logit)
        pulled = grad_mixed[:, here]
        total(2, pulled * rough)
        total(3, pulled)

    each(tail_front)
    sums_send[...] = jnp.zeros_like(sums_send)
    sums_send[pl.ds(4, 128, stride=8), :] = dot_nt(normed[...], d_logit[...])
    sums_send[pl.ds(5, 128, stride=8), :] = dot_nt(mixed[...], d_lifted[...])

    arrived(got_d, 3)
    assemble(got_d, turn)
    square[...] = dot_nt(right[...], turn[...])
    split(square, send_ga)
    send(send_ga, got_ga, 4)
    square[...] = dot(left[...], turn[...])
    split(square, send_gb)
    send(send_gb, got_gb, 5)

    def front_back(first, flat, keep, slope):
        def run(step, here):
            cells = gather(flat, step)
            d_front[first : first + 128, here] = (cells * keep[:, here]).astype(BF16)
            d_front[first + 128 : first + 256, here] = (cells * slope[:, here]).astype(BF16)

        return run

    arrived(got_ga, 4)
    flat_a[...] = got_ga[...].astype(F32)
    each(front_back(0, flat_a, keep_a, slope_a))
    arrived(got_gb, 5)
    flat_b[...] = got_gb[...].astype(F32)
    each(front_back(256, flat_b, keep_b, slope_b))

    def finish(step, here):
        pulled = tail_normed[:, here]
        for which, weight in enumerate((w_a_proj, w_a_gate, w_b_proj, w_b_gate)):
            pulled = pulled + dot(weight[...], d_front[128 * which : 128 * which + 128, here])
        rough = hat[:, here]
        total(0, pulled * rough)
        total(1, pulled)
        pulled = pulled * columns[0]
        back = scale[:, here] * (pulled - mean0(pulled) - rough * mean0(pulled * rough))
        turn_back(pair_grad, step, (cot_t[:, here] + back).astype(BF16))

    each(finish)
    weights_back = dot_nt(normed[...], d_front[...])
    for which in range(4):
        sums_send[pl.ds(which, 128, stride=8), :] = weights_back[:, 128 * which : 128 * which + 128]
    for which, at in enumerate((6, 7, 14, 15)):
        sums_send[at : at + 1] = jnp.sum(totals[which].T, axis=0, keepdims=True)

    own = pl.ds(pl.multiple_of(me * 8, 8), 8)

    def start_sum(step, carry):
        peer = lax.rem(me + step * ORDER, DEVICES)
        pltpu.make_async_remote_copy(
            src_ref=sums_send.at[pl.ds(pl.multiple_of(peer * 8, 8), 8)],
            dst_ref=sums_got.at[own],
            send_sem=send_sem.at[6],
            recv_sem=recv_sem.at[6],
            device_id=place(peer),
            device_id_type=pl.DeviceIdType.MESH,
        ).start()
        return carry

    lax.fori_loop(1, DEVICES, start_sum, 0)
    sums_got[own] = sums_send[own]
    arrived(sums_got, 6, (DEVICES - 1) * 8)
    share[...] = jnp.sum(sums_got[...].reshape(DEVICES, 8, 128), axis=0) * (1.0 / TOKENS)

    def start_share(step, carry):
        pltpu.make_async_remote_copy(
            src_ref=share,
            dst_ref=sums.at[own],
            send_sem=send_sem.at[7],
            recv_sem=recv_sem.at[7],
            device_id=place(lax.rem(me + step * ORDER, DEVICES)),
            device_id_type=pl.DeviceIdType.MESH,
        ).start()
        return carry

    lax.fori_loop(1, DEVICES, start_share, 0)
    sums[own] = share[...]
    for slot, source in enumerate((send_a, send_b, send_p, send_d, send_ga, send_gb)):
        left_device(source, slot)
    left_device(sums_send, 6, (DEVICES - 1) * 8)
    arrived(sums, 7, (DEVICES - 1) * 8)
    left_device(sums, 7, (DEVICES - 1) * 8)


def spread(tile):
    padded = jnp.pad(tile.reshape(TR, 2, TR, 128), ((0, 4), (0, 0), (0, 4), (0, 0)))
    return padded.reshape(2, 16, 64, 128).transpose(1, 0, 2, 3).reshape(16, 128, 128)


def gathered(cells):
    tile = cells.reshape(16, 2, 64, 128).transpose(1, 0, 2, 3).reshape(32, 2, 32, 128)
    return tile[:TR, :, :TR].reshape(TR, TC, 128)


def body(pair, cotangent, *rest):
    weights, vectors, drop_bits, tok_mask = rest[:6], rest[6:10], rest[10], rest[11]
    vmem = pltpu.VMEM
    blocks = [vmem((DEVICES * PART, 128), BF16)] * 12
    squares = [vmem((SIDE, SIDE), BF16)] * 3 + [vmem((SIDE, SIDE), F32)]
    flats = [vmem((DEVICES * PART, 128), F32)] * 2
    half, full = vmem((128, CELLS), BF16), vmem((128, CELLS), F32)
    scratch = blocks + squares + flats
    scratch += [vmem((128, 128), BF16), vmem((640, 128), BF16), vmem((128, 128), BF16)]
    scratch += [vmem((4, 128, WIDE), F32), vmem((32, 128), F32)]
    scratch += [half, full, vmem((1, CELLS), F32), full, full, full, full, full, full, full, full]
    scratch += [half, full, full, half, half, vmem((512, CELLS), BF16), full]
    scratch += [vmem((4, 128, 128), F32)] + [vmem((DEVICES * 8, 128), F32)] * 2
    scratch += [vmem((8, 128), F32)]
    scratch += [pltpu.SemaphoreType.DMA((8,)), pltpu.SemaphoreType.DMA((8,))]
    result, pair_grad, sums = pl.pallas_call(
        kernel,
        out_shape=(
            jax.ShapeDtypeStruct((16, 128, 128), BF16),
            jax.ShapeDtypeStruct((16, 128, 128), BF16),
            jax.ShapeDtypeStruct((DEVICES * 8, 128), F32),
        ),
        in_specs=[pl.BlockSpec(memory_space=vmem)] * 14,
        out_specs=[pl.BlockSpec(memory_space=vmem)] * 3,
        scratch_shapes=scratch,
        compiler_params=pltpu.CompilerParams(
            collective_id=0, has_side_effects=True, vmem_limit_bytes=50 * 2**20
        ),
    )(
        spread(pair),
        spread(cotangent),
        *weights,
        *(vector.reshape(1, 128) for vector in vectors),
        drop_bits,
        tok_mask.reshape(1, TOKENS),
    )
    sums = sums.reshape(DEVICES, 8, 128)
    return (
        (gathered(result), gathered(pair_grad))
        + tuple(sums[:, which] for which in range(6))
        + (sums[0, 6], sums[0, 7], sums[1, 6], sums[1, 7])
    )


def solution(mesh):
    tiles = P("row", "col", None)
    return jax.shard_map(
        body,
        mesh=mesh,
        in_specs=(tiles, tiles) + (P(),) * 10 + (P("row", None), P()),
        out_specs=(tiles, tiles) + (P(),) * 10,
        check_vma=False,
    )
```

```python
import jax
import jax.numpy as jnp
from jax import lax
from jax.experimental import pallas as pl
from jax.experimental.pallas import tpu as pltpu
from jax.sharding import PartitionSpec as P

LN_EPS = 1e-05
KEEP_RATE = 0.75
ROWS, COLS = 16, 8
DEVICES = ROWS * COLS
TR, TC = 28, 56
TOKENS = 448
WIDE = 256
STEPS = 7
CELLS = WIDE * STEPS
SIDE = 512
PART = 16
HALF = 14
ORDER = 45
OWNERS = DEVICES // 2
BF16 = jnp.bfloat16
F32 = jnp.float32


def dot(left, right):
    return jnp.dot(left, right, preferred_element_type=F32)


def dot_nt(left, right):
    return lax.dot_general(left, right, (((1,), (1,)), ((), ())), preferred_element_type=F32)


def dot_tn(left, right):
    return lax.dot_general(left, right, (((0,), (0,)), ((), ())), preferred_element_type=F32)


def mean0(values):
    return jnp.mean(values, axis=0, keepdims=True)


def swap_halves(first, second):
    low = lax.broadcasted_iota(jnp.int32, first.shape, 1) < 64
    turned_first = pltpu.roll(first, 64, 1)
    turned_second = pltpu.roll(second, 64, 1)
    return jnp.where(low, first, turned_second), jnp.where(low, turned_first, second)


def kernel(
    pair,
    cot,
    w_a_proj,
    w_a_gate,
    w_b_proj,
    w_b_gate,
    w_gate,
    w_out,
    in_gain,
    in_bias,
    mid_gain,
    mid_bias,
    drop,
    tok,
    result,
    pair_grad,
    sums,
    send_ab,
    send_p,
    send_d,
    send_ga,
    send_gb,
    got_ab,
    got_p,
    got_d,
    got_ga,
    got_gb,
    left,
    right,
    turn,
    square,
    flat_ab,
    flat_a,
    flat_b,
    eye,
    w_in_t,
    w_out_t,
    w_all,
    columns,
    drop_wide,
    stack,
    hat,
    scale,
    keep_a,
    slope_a,
    keep_b,
    slope_b,
    pair_t,
    cot_t,
    lift_keep,
    logit_keep,
    d_lifted,
    grad_mixed,
    mid_hat,
    mixed,
    d_all,
    totals,
    sums_flat,
    sums_send,
    sums_got,
    share,
    send_sem,
    recv_sem,
):
    row, col = lax.axis_index("row"), lax.axis_index("col")
    me = row * COLS + col
    barrier = pltpu.get_barrier_semaphore()

    def place(peer):
        return (peer // COLS, lax.rem(peer, COLS))

    def greet(step, carry):
        pl.semaphore_signal(
            barrier,
            inc=1,
            device_id=place(lax.rem(me + step, DEVICES)),
            device_id_type=pl.DeviceIdType.MESH,
        )
        return carry

    lax.fori_loop(1, DEVICES, greet, 0)

    def send(source, target, slot, size=PART):
        mine = pl.ds(pl.multiple_of(me * size, size), size)

        def start(step, carry):
            peer = lax.rem(me + step * ORDER, DEVICES)
            pltpu.make_async_remote_copy(
                src_ref=source.at[pl.ds(pl.multiple_of(peer * size, size), size)],
                dst_ref=target.at[mine],
                send_sem=send_sem.at[slot],
                recv_sem=recv_sem.at[slot],
                device_id=place(peer),
                device_id_type=pl.DeviceIdType.MESH,
            ).start()
            return carry

        lax.fori_loop(1, DEVICES, start, 0)
        target[mine] = source[mine]

    def settle(ref, sem, slot, length):
        some = ref.at[pl.ds(0, length)]
        pltpu.make_async_copy(some, some, sem.at[slot]).wait()

    def arrived(target, slot, size=PART):
        settle(target, recv_sem, slot, (DEVICES - 1) * size)

    def lanes(step):
        return pl.ds(pl.multiple_of(step * WIDE, WIDE), WIDE)

    def each(body):
        def run(step, carry):
            body(step, lanes(step))
            return carry

        lax.fori_loop(0, STEPS, run, 0, unroll=STEPS)

    def scatter(flat, step, values, stride=PART, shift=0):
        flat[pl.ds(2 * step + shift, 128, stride=stride), :] = values[:, :128]
        flat[pl.ds(2 * step + shift + 1, 128, stride=stride), :] = values[:, 128:]

    def gather(flat, step):
        return jnp.concatenate(
            [
                flat[pl.ds(2 * step, 128, stride=PART), :],
                flat[pl.ds(2 * step + 1, 128, stride=PART), :],
            ],
            axis=1,
        )

    def turned(ref, step):
        return jnp.concatenate(
            [dot_nt(eye[...], ref[2 * step]), dot_nt(eye[...], ref[2 * step + 1])], axis=1
        )

    def turn_back(ref, step, values):
        ref[2 * step] = dot_nt(eye[...], values[:, :128]).astype(BF16)
        ref[2 * step + 1] = dot_nt(eye[...], values[:, 128:]).astype(BF16)

    def assemble(blocks, matrix, stride=PART, shift=0):
        def run(index, carry):
            base = pl.multiple_of(index * COLS * stride, COLS * stride)
            top = pl.multiple_of(index * 32, 32)
            for pick in range(4):
                one = blocks[pl.ds(base + 2 * pick * stride + shift, PART)].astype(F32)
                two = blocks[pl.ds(base + (2 * pick + 1) * stride + shift, PART)].astype(F32)
                upper, lower = swap_halves(one, two)
                here = pl.ds(128 * pick, 128)
                matrix[pl.ds(top, PART), here] = upper.astype(BF16)
                matrix[pl.ds(top + PART, PART), here] = lower.astype(BF16)
            return carry

        lax.fori_loop(0, ROWS, run, 0, unroll=ROWS)

    def split(matrix, blocks):
        def run(index, carry):
            base = pl.multiple_of(index * 128, 128)
            top = pl.multiple_of(index * 32, 32)
            for pick in range(4):
                here = pl.ds(128 * pick, 128)
                upper = matrix[pl.ds(top, PART), here]
                lower = matrix[pl.ds(top + PART, PART), here]
                one, two = swap_halves(upper, lower)
                blocks[pl.ds(base + 32 * pick, PART)] = one.astype(BF16)
                blocks[pl.ds(base + 32 * pick + PART, PART)] = two.astype(BF16)
            return carry

        lax.fori_loop(0, ROWS, run, 0, unroll=ROWS)

    eye[...] = (
        lax.broadcasted_iota(jnp.int32, (128, 128), 0)
        == lax.broadcasted_iota(jnp.int32, (128, 128), 1)
    ).astype(BF16)
    for place_of, weight in enumerate((w_a_proj, w_a_gate, w_b_proj, w_b_gate, w_gate)):
        here = slice(128 * place_of, 128 * place_of + 128)
        w_in_t[here] = dot_nt(eye[...], weight[...]).astype(BF16)
        w_all[:, here] = weight[...]
    w_out_t[...] = dot_nt(eye[...], w_out[...]).astype(BF16)
    for place_of, vector in enumerate((in_gain, in_bias, mid_gain, mid_bias)):
        column = jnp.broadcast_to(vector[...], (128, 128)).T
        columns[place_of] = jnp.concatenate([column, column], axis=1)
    stack[256:272] = jnp.ones((16, CELLS), BF16)
    flat_ab[...] = jnp.zeros_like(flat_ab)
    flat_b[...] = jnp.zeros_like(flat_b)
    drop_wide[...] = jnp.zeros_like(drop_wide)
    drop_wide[0:TR] = drop[...].astype(F32)
    live = jnp.sum(tok[...].astype(F32), axis=1, keepdims=True)

    def cell_mask(step):
        lane = lax.broadcasted_iota(jnp.int32, (1, WIDE), 1)
        tile_row = ((lane >> 6) & 1) * HALF + (lane >> 7) + 2 * step
        within = lane & 15
        tile_col = ((lane >> 4) & 3) * HALF + within
        grid_row = (tile_row + row * TR).astype(F32)
        grid_col = (tile_col + col * TC).astype(F32)
        one = jnp.where(grid_row < live, 1.0, 0.0) * jnp.where(grid_col < live, 1.0, 0.0)
        return one * jnp.where(within < HALF, 1.0, 0.0)

    def front(step, here, weights, keep, slope, shift):
        logits = dot(w_in_t[weights], stack[0:128, here])
        squash = jax.nn.sigmoid(logits[128:])
        masked = squash * cell_mask(step)
        values = logits[:128] * masked
        keep[:, here] = masked
        slope[:, here] = values * (1.0 - squash)
        scatter(flat_ab, step, values, 2 * PART, shift)

    def front_a(step, here):
        cells = turned(pair, step)
        pair_t[:, here] = cells
        centered = cells - mean0(cells)
        root = lax.rsqrt(mean0(centered * centered) + LN_EPS)
        rough = centered * root
        hat[:, here] = rough
        scale[:, here] = root
        stack[0:128, here] = (rough * columns[0] + columns[1]).astype(BF16)
        stack[128:256, here] = rough.astype(BF16)
        front(step, here, slice(0, 256), keep_a, slope_a, 0)
        front(step, here, slice(256, 512), keep_b, slope_b, PART)

    each(front_a)
    send_ab[...] = flat_ab[...].astype(BF16)
    pl.semaphore_wait(barrier, DEVICES - 1)
    send(send_ab, got_ab, 0, 2 * PART)

    def prepare(step, here):
        squash = jax.nn.sigmoid(dot(w_in_t[512:640], stack[0:128, here]))
        lane = lax.broadcasted_iota(jnp.int32, (32, WIDE), 1)
        chosen = ((lane >> 6) & 1) * HALF + (lane >> 7) + 2 * step
        pick = (lax.broadcasted_iota(jnp.int32, (32, WIDE), 0) == chosen).astype(BF16)
        bits = dot_tn(drop_wide[...].astype(BF16), pick)
        kept = bits * (1.0 / KEEP_RATE)
        upstream = turned(cot, step)
        cot_t[:, here] = upstream
        lift_keep[:, here] = kept * squash
        pulled = upstream * kept * squash
        logit_keep[:, here] = pulled * (1.0 - squash)
        lifted_back = pulled.astype(BF16)
        d_lifted[:, here] = lifted_back
        grad_mixed[:, here] = dot(w_out[...], lifted_back)

    each(prepare)
    arrived(got_ab, 0, 2 * PART)
    assemble(got_ab, left, 2 * PART)
    assemble(got_ab, right, 2 * PART, PART)
    square[...] = dot_tn(left[...], right[...])
    split(square, send_p)
    send(send_p, got_p, 2)

    arrived(got_p, 2)
    flat_a[...] = got_p[...].astype(F32)

    def tail_back(step, here):
        cells = gather(flat_a, step)
        centered = cells - mean0(cells)
        root = lax.rsqrt(mean0(centered * centered) + LN_EPS)
        rough = centered * root
        mid_hat[:, here] = rough
        pulled = grad_mixed[:, here] * columns[2]
        scatter(flat_b, step, root * (pulled - mean0(pulled) - rough * mean0(pulled * rough)))

    each(tail_back)
    send_d[...] = flat_b[...].astype(BF16)
    send(send_d, got_d, 3)

    totals[...] = jnp.zeros_like(totals)

    def total(which, values):
        totals[which] += values[:, :128] + values[:, 128:]

    def tail_front(step, here):
        rough = mid_hat[:, here]
        blended = (rough * columns[2] + columns[3]).astype(BF16)
        mixed[:, here] = blended
        lifted = dot(w_out_t[...], blended)
        turn_back(result, step, (pair_t[:, here] + lift_keep[:, here] * lifted).astype(BF16))
        logit = (logit_keep[:, here] * lifted).astype(BF16)
        d_all[512:640, here] = logit
        pulled = grad_mixed[:, here]
        total(2, pulled * rough)
        total(3, pulled)

    each(tail_front)
    sums_flat[...] = jnp.zeros_like(sums_flat)

    def put_sums(which, values):
        sums_flat[pl.ds(which, OWNERS, stride=PART), :] = values[:OWNERS]
        sums_flat[pl.ds(which + 6, OWNERS, stride=PART), :] = values[OWNERS:]

    def put_front(first, last):
        outer = dot_nt(stack[...], d_all[128 * first : 128 * last])
        for which in range(first, last):
            here = slice(128 * (which - first), 128 * (which - first) + 128)
            put_sums(which, outer[0:128, here])
            weight = w_all[:, 128 * which : 128 * which + 128].astype(F32)
            totals[0] += outer[128:256, here] * weight
            totals[1] += outer[256:257, here] * weight

    def put_vector(which):
        sums_flat[12 + which : 13 + which] = jnp.sum(totals[which].T, axis=0, keepdims=True)

    put_front(4, 5)
    put_sums(5, dot_nt(mixed[...], d_lifted[...]))
    put_vector(2)
    put_vector(3)

    arrived(got_d, 3)
    assemble(got_d, turn)
    square[...] = dot_nt(right[...], turn[...])
    split(square, send_ga)
    send(send_ga, got_ga, 4)
    square[...] = dot(left[...], turn[...])
    split(square, send_gb)
    send(send_gb, got_gb, 5)

    def front_back(first, flat, keep, slope):
        def run(step, here):
            cells = gather(flat, step)
            d_all[first : first + 128, here] = (cells * keep[:, here]).astype(BF16)
            d_all[first + 128 : first + 256, here] = (cells * slope[:, here]).astype(BF16)

        return run

    arrived(got_ga, 4)
    flat_a[...] = got_ga[...].astype(F32)
    each(front_back(0, flat_a, keep_a, slope_a))
    put_front(0, 2)
    arrived(got_gb, 5)
    flat_b[...] = got_gb[...].astype(F32)
    each(front_back(256, flat_b, keep_b, slope_b))
    put_front(2, 4)
    put_vector(0)
    put_vector(1)
    sums_send[...] = sums_flat[...].astype(BF16)

    core = lax.rem(row, 2)
    chip = (row // 2) * COLS + col
    mine = pl.ds(pl.multiple_of(me * PART, PART), PART)
    owned = pl.ds(pl.multiple_of(chip * PART, PART), PART)

    def start_sum(step, carry):
        owner = lax.rem(chip + step * ORDER, OWNERS)
        pltpu.make_async_remote_copy(
            src_ref=sums_send.at[pl.ds(pl.multiple_of(owner * PART, PART), PART)],
            dst_ref=sums_got.at[mine],
            send_sem=send_sem.at[6],
            recv_sem=recv_sem.at[6],
            device_id=((owner // COLS) * 2, lax.rem(owner, COLS)),
            device_id_type=pl.DeviceIdType.MESH,
        ).start()
        return carry

    lax.fori_loop(1, OWNERS, start_sum, 0)

    @pl.when(core == 1)
    def _():
        start_sum(0, 0)

    def finish(step, here):
        pulled = dot(w_all[...], d_all[:, here]) * columns[0]
        rough = hat[:, here]
        back = scale[:, here] * (pulled - mean0(pulled) - rough * mean0(pulled * rough))
        turn_back(pair_grad, step, (cot_t[:, here] + back).astype(BF16))

    each(finish)

    @pl.when(core == 0)
    def _():
        sums_got[mine] = sums_send[owned]
        arrived(sums_got, 6)
        whole = jnp.sum(sums_got[...].astype(F32).reshape(DEVICES, PART, 128), axis=0)
        share[...] = (whole * (1.0 / TOKENS)).astype(BF16)

        def start_share(step, carry):
            pltpu.make_async_remote_copy(
                src_ref=share,
                dst_ref=sums.at[owned],
                send_sem=send_sem.at[7],
                recv_sem=recv_sem.at[7],
                device_id=place(lax.rem(me + step * ORDER, DEVICES)),
                device_id_type=pl.DeviceIdType.MESH,
            ).start()
            return carry

        lax.fori_loop(1, DEVICES, start_share, 0)
        sums[owned] = share[...]
        settle(sums, recv_sem, 7, (OWNERS - 1) * PART)
        settle(sums_got, send_sem, 7, (DEVICES - 1) * PART)
        settle(sums_send, send_sem, 6, (OWNERS - 1) * PART)

    @pl.when(core == 1)
    def _():
        settle(sums, recv_sem, 7, OWNERS * PART)
        settle(sums_send, send_sem, 6, OWNERS * PART)

    settle(send_ab, send_sem, 0, (DEVICES - 1) * 2 * PART)
    for slot, source in ((2, send_p), (3, send_d), (4, send_ga), (5, send_gb)):
        settle(source, send_sem, slot, (DEVICES - 1) * PART)


def spread(tile):
    padded = jnp.pad(tile.reshape(2, HALF, 4, HALF, 128), ((0, 0),) * 3 + ((0, 2), (0, 0)))
    return padded.transpose(1, 0, 2, 3, 4).reshape(HALF, 128, 128)


def gathered(cells):
    tile = cells.reshape(HALF, 2, 4, 16, 128)[:, :, :, :HALF].transpose(1, 0, 2, 3, 4)
    return tile.reshape(TR, TC, 128)


def body(pair, cotangent, *rest):
    weights, vectors, drop_bits, tok_mask = rest[:6], rest[6:10], rest[10], rest[11]
    vmem = pltpu.VMEM
    block, double = vmem((DEVICES * PART, 128), BF16), vmem((DEVICES * 2 * PART, 128), BF16)
    blocks = [double] + [block] * 4 + [double] + [block] * 4
    squares = [vmem((SIDE, SIDE), BF16)] * 3 + [vmem((SIDE, SIDE), F32)]
    flats = [vmem((DEVICES * 2 * PART, 128), F32)] + [vmem((DEVICES * PART, 128), F32)] * 2
    half, full = vmem((128, CELLS), BF16), vmem((128, CELLS), F32)
    scratch = blocks + squares + flats
    scratch += [vmem((128, 128), BF16), vmem((640, 128), BF16), vmem((128, 128), BF16)]
    scratch += [vmem((128, 640), BF16), vmem((4, 128, WIDE), F32), vmem((32, 128), F32)]
    scratch += [vmem((272, CELLS), BF16), full, vmem((1, CELLS), F32)] + [full] * 8
    scratch += [half, full, full, half, vmem((640, CELLS), BF16)]
    scratch += [vmem((4, 128, 128), F32), vmem((OWNERS * PART, 128), F32)]
    scratch += [vmem((OWNERS * PART, 128), BF16), block, vmem((PART, 128), BF16)]
    scratch += [pltpu.SemaphoreType.DMA((8,)), pltpu.SemaphoreType.DMA((8,))]
    result, pair_grad, sums = pl.pallas_call(
        kernel,
        out_shape=(
            jax.ShapeDtypeStruct((HALF, 128, 128), BF16),
            jax.ShapeDtypeStruct((HALF, 128, 128), BF16),
            jax.ShapeDtypeStruct((OWNERS * PART, 128), BF16),
        ),
        in_specs=[pl.BlockSpec(memory_space=vmem)] * 14,
        out_specs=[pl.BlockSpec(memory_space=vmem)] * 3,
        scratch_shapes=scratch,
        compiler_params=pltpu.CompilerParams(
            collective_id=0, has_side_effects=True, vmem_limit_bytes=50 * 2**20
        ),
    )(
        spread(pair),
        spread(cotangent),
        *weights,
        *(vector.reshape(1, 128) for vector in vectors),
        drop_bits,
        tok_mask.reshape(1, TOKENS),
    )
    sums = sums.reshape(OWNERS, PART, 128).astype(F32)
    return (
        (gathered(result), gathered(pair_grad))
        + tuple(
            jnp.concatenate([sums[:, which], sums[:, which + 6]], axis=0) for which in range(6)
        )
        + tuple(sums[0, 12 + which] for which in range(4))
    )


def solution(mesh):
    tiles = P("row", "col", None)
    return jax.shard_map(
        body,
        mesh=mesh,
        in_specs=(tiles, tiles) + (P(),) * 10 + (P("row", None), P()),
        out_specs=(tiles, tiles) + (P(),) * 10,
        check_vma=False,
    )
```

```python
import jax
import jax.numpy as jnp
from jax import lax
from jax.experimental import pallas as pl
from jax.experimental.pallas import tpu as pltpu
from jax.sharding import PartitionSpec as P

LN_EPS = 1e-05
KEEP_RATE = 0.75
ROWS, COLS = 16, 8
DEVICES = ROWS * COLS
TR, TC = 28, 56
TOKENS = 448
WIDE = 256
STEPS = 7
CELLS = WIDE * STEPS
SIDE = 512
PART = 16
HALF = 14
OWNERS = DEVICES // 2
BF16 = jnp.bfloat16
F32 = jnp.float32


def partners(cores):
    offsets = [
        (x, y, z, core)
        for x in range(4)
        for y in range(4)
        for z in range(4)
        for core in range(cores)
        if x or y or z or core
    ]

    def rank(offset):
        far = sum(min(step, 4 - step) for step in offset[:3])
        x, y, z, core = offset
        return -far, (29 * x + 13 * y + 7 * z + 17 * core) % 31, offset

    return sorted(offsets, key=rank)


def dot(left, right):
    return jnp.dot(left, right, preferred_element_type=F32)


def dot_nt(left, right):
    return lax.dot_general(left, right, (((1,), (1,)), ((), ())), preferred_element_type=F32)


def dot_tn(left, right):
    return lax.dot_general(left, right, (((0,), (0,)), ((), ())), preferred_element_type=F32)


def mean0(values):
    return jnp.mean(values, axis=0, keepdims=True)


def swap_halves(first, second):
    low = lax.broadcasted_iota(jnp.int32, first.shape, 1) < 64
    turned_first = pltpu.roll(first, 64, 1)
    turned_second = pltpu.roll(second, 64, 1)
    return jnp.where(low, first, turned_second), jnp.where(low, turned_first, second)


def kernel(*refs):
    inputs, refs = refs[:14], refs[14:]
    outputs, refs = refs[:3], refs[3:]
    run_kernel(inputs, outputs, refs[:8], *refs[8:])


def run_kernel(
    inputs,
    outputs,
    local,
    result_cells,
    grad_cells,
    pick_cells,
    sums,
    send_ab,
    send_p,
    send_d,
    send_ga,
    send_gb,
    got_ab,
    got_p,
    got_d,
    got_ga,
    got_gb,
    left,
    right,
    turn,
    square,
    flat_ab,
    flat_a,
    flat_b,
    eye,
    w_in_t,
    w_out_t,
    w_all,
    columns,
    drop_wide,
    stack,
    hat,
    scale,
    keep_a,
    slope_a,
    keep_b,
    slope_b,
    pair_t,
    cot_t,
    lift_keep,
    logit_keep,
    d_lifted,
    grad_mixed,
    mid_hat,
    mixed,
    d_all,
    totals,
    sums_flat,
    sums_send,
    sums_got,
    share,
    send_sem,
    recv_sem,
    local_sem,
):
    in_gain, in_bias, mid_gain, mid_bias, drop, tok = inputs[8:]
    result, pair_grad, all_sums = outputs
    pair, cot, w_a_proj, w_a_gate, w_b_proj, w_b_gate, w_gate, w_out = local
    fetches = [
        pltpu.make_async_copy(inputs[which], local[which], local_sem.at[which])
        for which in range(8)
    ]
    for fetch in fetches:
        fetch.start()
    row, col = lax.axis_index("row"), lax.axis_index("col")
    me = row * COLS + col
    barrier = pltpu.get_barrier_semaphore()

    def place(peer):
        return (peer // COLS, lax.rem(peer, COLS))

    def greet(step, carry):
        pl.semaphore_signal(
            barrier,
            inc=1,
            device_id=place(lax.rem(me + step, DEVICES)),
            device_id_type=pl.DeviceIdType.MESH,
        )
        return carry

    lax.fori_loop(1, DEVICES, greet, 0)

    core = lax.rem(row, 2)
    at_x, at_y, at_z = lax.rem(row // 2, 2) * 2 + col // 4, row // 4, lax.rem(col, 4)
    steps_x = [lax.rem(at_x + step, 4) for step in range(4)]
    part_x = [(step // 2) * 16 + lax.rem(step, 2) * 4 for step in steps_x]
    part_y = [lax.rem(at_y + step, 4) * 32 for step in range(4)]
    part_z = [lax.rem(at_z + step, 4) for step in range(4)]
    part_core = [lax.rem(core + step, 2) * 8 for step in range(2)]

    def device_at(x, y, z, other_core):
        return part_x[x] + part_y[y] + part_z[z] + part_core[other_core]

    def send(source, target, slot, size=PART):
        mine = pl.ds(pl.multiple_of(me * size, size), size)

        for offset in partners(2):
            peer = device_at(*offset)
            pltpu.make_async_remote_copy(
                src_ref=source.at[pl.ds(pl.multiple_of(peer * size, size), size)],
                dst_ref=target.at[mine],
                send_sem=send_sem.at[slot],
                recv_sem=recv_sem.at[slot],
                device_id=place(peer),
                device_id_type=pl.DeviceIdType.MESH,
            ).start()
        target[mine] = source[mine]

    def settle(ref, sem, slot, length):
        some = ref.at[pl.ds(0, length)]
        pltpu.make_async_copy(some, some, sem.at[slot]).wait()

    def arrived(target, slot, size=PART):
        settle(target, recv_sem, slot, (DEVICES - 1) * size)

    def lanes(step):
        return pl.ds(pl.multiple_of(step * WIDE, WIDE), WIDE)

    def each(body):
        def run(step, carry):
            body(step, lanes(step))
            return carry

        lax.fori_loop(0, STEPS, run, 0, unroll=STEPS)

    def scatter(flat, step, values, stride=PART, shift=0):
        flat[pl.ds(2 * step + shift, 128, stride=stride), :] = values[:, :128]
        flat[pl.ds(2 * step + shift + 1, 128, stride=stride), :] = values[:, 128:]

    def gather(flat, step):
        return jnp.concatenate(
            [
                flat[pl.ds(2 * step, 128, stride=PART), :],
                flat[pl.ds(2 * step + 1, 128, stride=PART), :],
            ],
            axis=1,
        )

    def tile_rows(step, part):
        first = pl.multiple_of((2 * step + part) * TC, 8)
        second = pl.multiple_of((2 * step + part + HALF) * TC, 8)
        return pl.ds(first, TC), pl.ds(second, TC)

    def turned(ref, step):
        parts = []
        for part in range(2):
            first, second = tile_rows(step, part)
            cells = jnp.concatenate([ref[first], ref[second]], axis=0).astype(BF16)
            parts.append(dot_tn(cells, pick_cells[...]))
        return jnp.concatenate(parts, axis=1)

    def turn_back(ref, step, values):
        for part in range(2):
            first, second = tile_rows(step, part)
            cells = dot_nt(pick_cells[...], values[:, 128 * part : 128 * part + 128])
            ref[first] = cells[:TC]
            ref[second] = cells[TC:]

    def assemble(blocks, matrix, stride=PART, shift=0):
        def run(index, carry):
            base = pl.multiple_of(index * COLS * stride, COLS * stride)
            top = pl.multiple_of(index * 32, 32)
            for pick in range(4):
                one = blocks[pl.ds(base + 2 * pick * stride + shift, PART)].astype(F32)
                two = blocks[pl.ds(base + (2 * pick + 1) * stride + shift, PART)].astype(F32)
                upper, lower = swap_halves(one, two)
                here = pl.ds(128 * pick, 128)
                matrix[pl.ds(top, PART), here] = upper.astype(BF16)
                matrix[pl.ds(top + PART, PART), here] = lower.astype(BF16)
            return carry

        lax.fori_loop(0, ROWS, run, 0, unroll=ROWS)

    def split(matrix, blocks):
        def run(index, carry):
            base = pl.multiple_of(index * 128, 128)
            top = pl.multiple_of(index * 32, 32)
            for pick in range(4):
                here = pl.ds(128 * pick, 128)
                upper = matrix[pl.ds(top, PART), here]
                lower = matrix[pl.ds(top + PART, PART), here]
                one, two = swap_halves(upper, lower)
                blocks[pl.ds(base + 32 * pick, PART)] = one.astype(BF16)
                blocks[pl.ds(base + 32 * pick + PART, PART)] = two.astype(BF16)
            return carry

        lax.fori_loop(0, ROWS, run, 0, unroll=ROWS)

    eye[...] = (
        lax.broadcasted_iota(jnp.int32, (128, 128), 0)
        == lax.broadcasted_iota(jnp.int32, (128, 128), 1)
    ).astype(BF16)
    lane = lax.broadcasted_iota(jnp.int32, (2 * TC, 128), 1)
    wanted = (lane >> 6) * TC + ((lane >> 4) & 3) * HALF + (lane & 15)
    chosen_cell = lax.broadcasted_iota(jnp.int32, (2 * TC, 128), 0) == wanted
    chosen_cell = jnp.where(chosen_cell, 1.0, 0.0) * jnp.where((lane & 15) < HALF, 1.0, 0.0)
    pick_cells[...] = chosen_cell.astype(BF16)
    for fetch in fetches:
        fetch.wait()
    for place_of, weight in enumerate((w_a_proj, w_a_gate, w_b_proj, w_b_gate, w_gate)):
        here = slice(128 * place_of, 128 * place_of + 128)
        w_in_t[here] = dot_nt(eye[...], weight[...]).astype(BF16)
        w_all[:, here] = weight[...]
    w_out_t[...] = dot_nt(eye[...], w_out[...]).astype(BF16)
    for place_of, vector in enumerate((in_gain, in_bias, mid_gain, mid_bias)):
        column = jnp.broadcast_to(vector[...], (128, 128)).T
        columns[place_of] = jnp.concatenate([column, column], axis=1)
    stack[256:272] = jnp.ones((16, CELLS), BF16)
    flat_ab[...] = jnp.zeros_like(flat_ab)
    flat_b[...] = jnp.zeros_like(flat_b)
    drop_wide[...] = jnp.zeros_like(drop_wide)
    drop_wide[0:TR] = drop[...].astype(F32)
    live = jnp.sum(tok[...].astype(F32), axis=1, keepdims=True)

    def cell_mask(step):
        lane = lax.broadcasted_iota(jnp.int32, (1, WIDE), 1)
        tile_row = ((lane >> 6) & 1) * HALF + (lane >> 7) + 2 * step
        within = lane & 15
        tile_col = ((lane >> 4) & 3) * HALF + within
        grid_row = (tile_row + row * TR).astype(F32)
        grid_col = (tile_col + col * TC).astype(F32)
        one = jnp.where(grid_row < live, 1.0, 0.0) * jnp.where(grid_col < live, 1.0, 0.0)
        return one * jnp.where(within < HALF, 1.0, 0.0)

    def front(step, here, weights, keep, slope, shift):
        logits = dot(w_in_t[weights], stack[0:128, here])
        squash = jax.nn.sigmoid(logits[128:])
        masked = squash * cell_mask(step)
        values = logits[:128] * masked
        keep[:, here] = masked
        slope[:, here] = values * (1.0 - squash)
        scatter(flat_ab, step, values, 2 * PART, shift)

    def front_a(step, here):
        cells = turned(result_cells, step)
        pair_t[:, here] = cells
        centered = cells - mean0(cells)
        root = lax.rsqrt(mean0(centered * centered) + LN_EPS)
        rough = centered * root
        hat[:, here] = rough
        scale[:, here] = root
        stack[0:128, here] = (rough * columns[0] + columns[1]).astype(BF16)
        stack[128:256, here] = rough.astype(BF16)
        front(step, here, slice(0, 256), keep_a, slope_a, 0)
        front(step, here, slice(256, 512), keep_b, slope_b, PART)

    result_cells[...] = pair[...].astype(F32)
    each(front_a)
    send_ab[...] = flat_ab[...].astype(BF16)
    pl.semaphore_wait(barrier, DEVICES - 1)
    send(send_ab, got_ab, 0, 2 * PART)

    def prepare(step, here):
        squash = jax.nn.sigmoid(dot(w_in_t[512:640], stack[0:128, here]))
        lane = lax.broadcasted_iota(jnp.int32, (32, WIDE), 1)
        chosen = ((lane >> 6) & 1) * HALF + (lane >> 7) + 2 * step
        pick = (lax.broadcasted_iota(jnp.int32, (32, WIDE), 0) == chosen).astype(BF16)
        bits = dot_tn(drop_wide[...].astype(BF16), pick)
        kept = bits * (1.0 / KEEP_RATE)
        upstream = turned(grad_cells, step)
        cot_t[:, here] = upstream
        lift_keep[:, here] = kept * squash
        pulled = upstream * kept * squash
        logit_keep[:, here] = pulled * (1.0 - squash)
        lifted_back = pulled.astype(BF16)
        d_lifted[:, here] = lifted_back
        grad_mixed[:, here] = dot(w_out[...], lifted_back)

    grad_cells[...] = cot[...].astype(F32)
    each(prepare)
    arrived(got_ab, 0, 2 * PART)
    assemble(got_ab, left, 2 * PART)
    assemble(got_ab, right, 2 * PART, PART)
    square[...] = dot_tn(left[...], right[...])
    split(square, send_p)
    send(send_p, got_p, 2)

    arrived(got_p, 2)
    flat_a[...] = got_p[...].astype(F32)

    def tail_back(step, here):
        cells = gather(flat_a, step)
        centered = cells - mean0(cells)
        root = lax.rsqrt(mean0(centered * centered) + LN_EPS)
        rough = centered * root
        mid_hat[:, here] = rough
        pulled = grad_mixed[:, here] * columns[2]
        scatter(flat_b, step, root * (pulled - mean0(pulled) - rough * mean0(pulled * rough)))

    each(tail_back)
    send_d[...] = flat_b[...].astype(BF16)
    send(send_d, got_d, 3)

    totals[...] = jnp.zeros_like(totals)

    def total(which, values):
        totals[which] += values[:, :128] + values[:, 128:]

    def tail_front(step, here):
        rough = mid_hat[:, here]
        blended = (rough * columns[2] + columns[3]).astype(BF16)
        mixed[:, here] = blended
        lifted = dot(w_out_t[...], blended)
        turn_back(result_cells, step, (pair_t[:, here] + lift_keep[:, here] * lifted).astype(BF16))
        logit = (logit_keep[:, here] * lifted).astype(BF16)
        d_all[512:640, here] = logit
        pulled = grad_mixed[:, here]
        total(2, pulled * rough)
        total(3, pulled)

    each(tail_front)
    result[...] = result_cells[...].astype(BF16)
    sums_flat[...] = jnp.zeros_like(sums_flat)

    def put_sums(which, values):
        sums_flat[pl.ds(which, OWNERS, stride=PART), :] = values[:OWNERS]
        sums_flat[pl.ds(which + 6, OWNERS, stride=PART), :] = values[OWNERS:]

    def put_front(first, last):
        outer = dot_nt(stack[...], d_all[128 * first : 128 * last])
        for which in range(first, last):
            here = slice(128 * (which - first), 128 * (which - first) + 128)
            put_sums(which, outer[0:128, here])
            weight = w_all[:, 128 * which : 128 * which + 128].astype(F32)
            totals[0] += outer[128:256, here] * weight
            totals[1] += outer[256:257, here] * weight

    def put_vector(which):
        sums_flat[12 + which : 13 + which] = jnp.sum(totals[which].T, axis=0, keepdims=True)

    put_front(4, 5)
    put_sums(5, dot_nt(mixed[...], d_lifted[...]))
    put_vector(2)
    put_vector(3)

    arrived(got_d, 3)
    assemble(got_d, turn)
    square[...] = dot_nt(right[...], turn[...])
    split(square, send_ga)
    send(send_ga, got_ga, 4)
    square[...] = dot(left[...], turn[...])
    split(square, send_gb)
    send(send_gb, got_gb, 5)

    def front_back(first, flat, keep, slope):
        def run(step, here):
            cells = gather(flat, step)
            d_all[first : first + 128, here] = (cells * keep[:, here]).astype(BF16)
            d_all[first + 128 : first + 256, here] = (cells * slope[:, here]).astype(BF16)

        return run

    arrived(got_ga, 4)
    flat_a[...] = got_ga[...].astype(F32)
    each(front_back(0, flat_a, keep_a, slope_a))
    put_front(0, 2)
    arrived(got_gb, 5)
    flat_b[...] = got_gb[...].astype(F32)
    each(front_back(256, flat_b, keep_b, slope_b))
    put_front(2, 4)
    put_vector(0)
    put_vector(1)
    sums_send[...] = sums_flat[...].astype(BF16)

    chip = (row // 2) * COLS + col
    mine = pl.ds(pl.multiple_of(me * PART, PART), PART)
    owned = pl.ds(pl.multiple_of(chip * PART, PART), PART)

    def start_sum(x, y, z):
        home = part_x[x] + part_y[y] + part_z[z]
        owner = (home // 16) * COLS + lax.rem(home, COLS)
        pltpu.make_async_remote_copy(
            src_ref=sums_send.at[pl.ds(pl.multiple_of(owner * PART, PART), PART)],
            dst_ref=sums_got.at[mine],
            send_sem=send_sem.at[6],
            recv_sem=recv_sem.at[6],
            device_id=place(home),
            device_id_type=pl.DeviceIdType.MESH,
        ).start()

    for x, y, z, _ in partners(1):
        start_sum(x, y, z)

    @pl.when(core == 1)
    def _():
        start_sum(0, 0, 0)

    def finish(step, here):
        pulled = dot(w_all[...], d_all[:, here]) * columns[0]
        rough = hat[:, here]
        back = scale[:, here] * (pulled - mean0(pulled) - rough * mean0(pulled * rough))
        turn_back(grad_cells, step, (cot_t[:, here] + back).astype(BF16))

    each(finish)
    pair_grad[...] = grad_cells[...].astype(BF16)

    @pl.when(core == 0)
    def _():
        sums_got[mine] = sums_send[owned]
        arrived(sums_got, 6)
        whole = jnp.sum(sums_got[...].astype(F32).reshape(DEVICES, PART, 128), axis=0)
        share[...] = (whole * (1.0 / TOKENS)).astype(BF16)

        for offset in partners(2):
            pltpu.make_async_remote_copy(
                src_ref=share,
                dst_ref=sums.at[owned],
                send_sem=send_sem.at[7],
                recv_sem=recv_sem.at[7],
                device_id=place(device_at(*offset)),
                device_id_type=pl.DeviceIdType.MESH,
            ).start()

        sums[owned] = share[...]
        settle(sums, recv_sem, 7, (OWNERS - 1) * PART)
        settle(sums_got, send_sem, 7, (DEVICES - 1) * PART)
        settle(sums_send, send_sem, 6, (OWNERS - 1) * PART)

    @pl.when(core == 1)
    def _():
        settle(sums, recv_sem, 7, OWNERS * PART)
        settle(sums_send, send_sem, 6, OWNERS * PART)

    all_sums[...] = sums[...].astype(F32)
    settle(send_ab, send_sem, 0, (DEVICES - 1) * 2 * PART)
    for slot, source in ((2, send_p), (3, send_d), (4, send_ga), (5, send_gb)):
        settle(source, send_sem, slot, (DEVICES - 1) * PART)


def hand_out(result, pair_grad, sums, *outputs):
    outputs[0][...] = result[...]
    outputs[1][...] = pair_grad[...]
    for which in range(6):
        outputs[2 + which][0:OWNERS] = sums[pl.ds(which, OWNERS, stride=PART), :]
        outputs[2 + which][OWNERS:] = sums[pl.ds(which + 6, OWNERS, stride=PART), :]
    for which in range(4):
        outputs[8 + which][...] = sums[12 + which : 13 + which]


def body(pair, cotangent, *rest):
    weights, vectors, drop_bits, tok_mask = rest[:6], rest[6:10], rest[10], rest[11]
    vmem = pltpu.VMEM
    block, double = vmem((DEVICES * PART, 128), BF16), vmem((DEVICES * 2 * PART, 128), BF16)
    blocks = [double] + [block] * 4 + [double] + [block] * 4
    squares = [vmem((SIDE, SIDE), BF16)] * 3 + [vmem((SIDE, SIDE), F32)]
    flats = [vmem((DEVICES * 2 * PART, 128), F32)] + [vmem((DEVICES * PART, 128), F32)] * 2
    half, full = vmem((128, CELLS), BF16), vmem((128, CELLS), F32)
    square, tile = vmem((128, 128), BF16), (TR * TC, 128)
    scratch = [vmem(tile, BF16)] * 2 + [square] * 6 + [vmem(tile, F32)] * 2
    scratch += [vmem((2 * TC, 128), BF16), vmem((OWNERS * PART, 128), BF16)]
    scratch += blocks + squares + flats
    scratch += [vmem((128, 128), BF16), vmem((640, 128), BF16), vmem((128, 128), BF16)]
    scratch += [vmem((128, 640), BF16), vmem((4, 128, WIDE), F32), vmem((32, 128), F32)]
    scratch += [vmem((272, CELLS), BF16), full, vmem((1, CELLS), F32)] + [full] * 8
    scratch += [half, full, full, half, vmem((640, CELLS), BF16)]
    scratch += [vmem((4, 128, 128), F32), vmem((OWNERS * PART, 128), F32)]
    scratch += [vmem((OWNERS * PART, 128), BF16), block, vmem((PART, 128), BF16)]
    scratch += [pltpu.SemaphoreType.DMA((8,))] * 3
    done = pl.pallas_call(
        kernel,
        out_shape=[
            jax.ShapeDtypeStruct(tile, BF16),
            jax.ShapeDtypeStruct(tile, BF16),
            jax.ShapeDtypeStruct((OWNERS * PART, 128), F32),
        ],
        in_specs=[pl.BlockSpec(memory_space=pl.ANY)] * 8 + [pl.BlockSpec(memory_space=vmem)] * 6,
        out_specs=[pl.BlockSpec(memory_space=vmem)] * 3,
        scratch_shapes=scratch,
        compiler_params=pltpu.CompilerParams(
            collective_id=0, has_side_effects=True, vmem_limit_bytes=60 * 2**20
        ),
    )(
        pair.reshape(tile),
        cotangent.reshape(tile),
        *weights,
        *(vector.reshape(1, 128) for vector in vectors),
        drop_bits,
        tok_mask.reshape(1, TOKENS),
    )
    outs = pl.pallas_call(
        hand_out,
        out_shape=[jax.ShapeDtypeStruct(tile, BF16)] * 2
        + [jax.ShapeDtypeStruct((128, 128), F32)] * 6
        + [jax.ShapeDtypeStruct((1, 128), F32)] * 4,
        in_specs=[pl.BlockSpec(memory_space=vmem)] * 3,
        out_specs=[pl.BlockSpec(memory_space=vmem)] * 12,
        compiler_params=pltpu.CompilerParams(vmem_limit_bytes=60 * 2**20),
    )(*done)
    result, pair_grad = outs[0].reshape(TR, TC, 128), outs[1].reshape(TR, TC, 128)
    return (result, pair_grad) + tuple(outs[2:8]) + tuple(out.reshape(128) for out in outs[8:])


def solution(mesh):
    tiles = P("row", "col", None)
    return jax.shard_map(
        body,
        mesh=mesh,
        in_specs=(tiles, tiles) + (P(),) * 10 + (P("row", None), P()),
        out_specs=(tiles, tiles) + (P(),) * 10,
        check_vma=False,
    )
```

```python
import jax
import jax.numpy as jnp
from jax import lax
from jax.experimental import pallas as pl
from jax.experimental.pallas import tpu as pltpu
from jax.sharding import PartitionSpec as P

LN_EPS = 1e-05
KEEP_RATE = 0.75
ROWS, COLS = 16, 8
DEVICES = ROWS * COLS
TR, TC = 28, 56
TOKENS = 448
WIDE = 256
STEPS = 7
CELLS = WIDE * STEPS
SIDE = 512
PART = 16
HALF = 14
OWNERS = DEVICES // 2
BF16 = jnp.bfloat16
F32 = jnp.float32


def partners(cores):
    offsets = [
        (x, y, z, core)
        for x in range(4)
        for y in range(4)
        for z in range(4)
        for core in range(cores)
        if x or y or z or core
    ]

    def rank(offset):
        far = sum(min(step, 4 - step) for step in offset[:3])
        x, y, z, core = offset
        return -far, (29 * x + 13 * y + 7 * z + 17 * core) % 31, offset

    return sorted(offsets, key=rank)


def dot(left, right):
    return jnp.dot(left, right, preferred_element_type=F32)


def dot_nt(left, right):
    return lax.dot_general(left, right, (((1,), (1,)), ((), ())), preferred_element_type=F32)


def dot_tn(left, right):
    return lax.dot_general(left, right, (((0,), (0,)), ((), ())), preferred_element_type=F32)


def mean0(values):
    return jnp.mean(values, axis=0, keepdims=True)


def swap_halves(first, second):
    low = lax.broadcasted_iota(jnp.int32, first.shape, 1) < 64
    turned_first = pltpu.roll(first, 64, 1)
    turned_second = pltpu.roll(second, 64, 1)
    return jnp.where(low, first, turned_second), jnp.where(low, turned_first, second)


def kernel(*refs):
    inputs, refs = refs[:14], refs[14:]
    outputs, refs = refs[:3], refs[3:]
    run_kernel(inputs, outputs, refs[:14], *refs[14:])


def run_kernel(
    inputs,
    outputs,
    local,
    result_cells,
    grad_cells,
    pick_cells,
    sums,
    send_a,
    send_b,
    send_p,
    send_d,
    send_ga,
    send_gb,
    got_a,
    got_b,
    got_p,
    got_d,
    got_ga,
    got_gb,
    left,
    right,
    turn,
    square,
    flat_a,
    flat_b,
    eye,
    w_in_t,
    w_out_t,
    w_all,
    columns,
    drop_wide,
    stack,
    hat,
    scale,
    keep_a,
    slope_a,
    keep_b,
    slope_b,
    pair_t,
    cot_t,
    lift_keep,
    logit_keep,
    d_lifted,
    grad_mixed,
    mid_hat,
    mixed,
    d_all,
    totals,
    sums_flat,
    sums_send,
    sums_got,
    share,
    send_sem,
    recv_sem,
    local_sem,
):
    result, pair_grad, all_sums = outputs
    pair, cot, w_a_proj, w_a_gate, w_b_proj, w_b_gate, w_gate, w_out = local[:8]
    in_gain, in_bias, mid_gain, mid_bias, drop, tok = local[8:]
    fetches = [
        pltpu.make_async_copy(inputs[which], local[which], local_sem.at[which])
        for which in range(14)
    ]
    for fetch in fetches:
        fetch.start()
    row, col = lax.axis_index("row"), lax.axis_index("col")
    me = row * COLS + col
    barrier = pltpu.get_barrier_semaphore()

    def place(peer):
        return (peer // COLS, lax.rem(peer, COLS))

    def greet(step, carry):
        pl.semaphore_signal(
            barrier,
            inc=1,
            device_id=place(lax.rem(me + step, DEVICES)),
            device_id_type=pl.DeviceIdType.MESH,
        )
        return carry

    lax.fori_loop(1, DEVICES, greet, 0)

    core = lax.rem(row, 2)
    at_x, at_y, at_z = lax.rem(row // 2, 2) * 2 + col // 4, row // 4, lax.rem(col, 4)
    steps_x = [lax.rem(at_x + step, 4) for step in range(4)]
    part_x = [(step // 2) * 16 + lax.rem(step, 2) * 4 for step in steps_x]
    part_y = [lax.rem(at_y + step, 4) * 32 for step in range(4)]
    part_z = [lax.rem(at_z + step, 4) for step in range(4)]
    part_core = [lax.rem(core + step, 2) * 8 for step in range(2)]

    def device_at(x, y, z, other_core):
        return part_x[x] + part_y[y] + part_z[z] + part_core[other_core]

    def send(source, target, slot, size=PART):
        mine = pl.ds(pl.multiple_of(me * size, size), size)

        for offset in partners(2):
            peer = device_at(*offset)
            pltpu.make_async_remote_copy(
                src_ref=source.at[pl.ds(pl.multiple_of(peer * size, size), size)],
                dst_ref=target.at[mine],
                send_sem=send_sem.at[slot],
                recv_sem=recv_sem.at[slot],
                device_id=place(peer),
                device_id_type=pl.DeviceIdType.MESH,
            ).start()
        target[mine] = source[mine]

    def settle(ref, sem, slot, length):
        some = ref.at[pl.ds(0, length)]
        pltpu.make_async_copy(some, some, sem.at[slot]).wait()

    def arrived(target, slot, size=PART):
        settle(target, recv_sem, slot, (DEVICES - 1) * size)

    def lanes(step):
        return pl.ds(pl.multiple_of(step * WIDE, WIDE), WIDE)

    def each(body):
        def run(step, carry):
            body(step, lanes(step))
            return carry

        lax.fori_loop(0, STEPS, run, 0, unroll=STEPS)

    def scatter(flat, step, values, stride=PART, shift=0):
        flat[pl.ds(2 * step + shift, 128, stride=stride), :] = values[:, :128]
        flat[pl.ds(2 * step + shift + 1, 128, stride=stride), :] = values[:, 128:]

    def gather(flat, step):
        return jnp.concatenate(
            [
                flat[pl.ds(2 * step, 128, stride=PART), :],
                flat[pl.ds(2 * step + 1, 128, stride=PART), :],
            ],
            axis=1,
        )

    def tile_rows(step, part):
        first = pl.multiple_of((2 * step + part) * TC, 8)
        second = pl.multiple_of((2 * step + part + HALF) * TC, 8)
        return pl.ds(first, TC), pl.ds(second, TC)

    def turned(ref, step):
        parts = []
        for part in range(2):
            first, second = tile_rows(step, part)
            cells = jnp.concatenate([ref[first], ref[second]], axis=0).astype(BF16)
            parts.append(dot_tn(cells, pick_cells[...]))
        return jnp.concatenate(parts, axis=1)

    def turn_back(ref, step, values):
        for part in range(2):
            first, second = tile_rows(step, part)
            cells = dot_nt(pick_cells[...], values[:, 128 * part : 128 * part + 128])
            ref[first] = cells[:TC]
            ref[second] = cells[TC:]

    def assemble(blocks, matrix, stride=PART, shift=0):
        def run(index, carry):
            base = pl.multiple_of(index * COLS * stride, COLS * stride)
            top = pl.multiple_of(index * 32, 32)
            for pick in range(4):
                one = blocks[pl.ds(base + 2 * pick * stride + shift, PART)].astype(F32)
                two = blocks[pl.ds(base + (2 * pick + 1) * stride + shift, PART)].astype(F32)
                upper, lower = swap_halves(one, two)
                here = pl.ds(128 * pick, 128)
                matrix[pl.ds(top, PART), here] = upper.astype(BF16)
                matrix[pl.ds(top + PART, PART), here] = lower.astype(BF16)
            return carry

        lax.fori_loop(0, ROWS, run, 0, unroll=ROWS)

    def split(matrix, blocks):
        def run(index, carry):
            base = pl.multiple_of(index * 128, 128)
            top = pl.multiple_of(index * 32, 32)
            for pick in range(4):
                here = pl.ds(128 * pick, 128)
                upper = matrix[pl.ds(top, PART), here]
                lower = matrix[pl.ds(top + PART, PART), here]
                one, two = swap_halves(upper, lower)
                blocks[pl.ds(base + 32 * pick, PART)] = one.astype(BF16)
                blocks[pl.ds(base + 32 * pick + PART, PART)] = two.astype(BF16)
            return carry

        lax.fori_loop(0, ROWS, run, 0, unroll=ROWS)

    flat_a[...] = jnp.zeros_like(flat_a)
    flat_b[...] = jnp.zeros_like(flat_b)
    stack[256:272] = jnp.ones((16, CELLS), BF16)
    eye[...] = (
        lax.broadcasted_iota(jnp.int32, (128, 128), 0)
        == lax.broadcasted_iota(jnp.int32, (128, 128), 1)
    ).astype(BF16)
    lane = lax.broadcasted_iota(jnp.int32, (2 * TC, 128), 1)
    wanted = (lane >> 6) * TC + ((lane >> 4) & 3) * HALF + (lane & 15)
    chosen_cell = lax.broadcasted_iota(jnp.int32, (2 * TC, 128), 0) == wanted
    chosen_cell = jnp.where(chosen_cell, 1.0, 0.0) * jnp.where((lane & 15) < HALF, 1.0, 0.0)
    pick_cells[...] = chosen_cell.astype(BF16)
    for fetch in fetches:
        fetch.wait()
    for place_of, weight in enumerate((w_a_proj, w_a_gate, w_b_proj, w_b_gate, w_gate)):
        here = slice(128 * place_of, 128 * place_of + 128)
        w_in_t[here] = dot_nt(eye[...], weight[...]).astype(BF16)
        w_all[:, here] = weight[...]
    w_out_t[...] = dot_nt(eye[...], w_out[...]).astype(BF16)
    for place_of, vector in enumerate((in_gain, in_bias, mid_gain, mid_bias)):
        column = jnp.broadcast_to(vector[...], (128, 128)).T
        columns[place_of] = jnp.concatenate([column, column], axis=1)
    drop_wide[...] = jnp.zeros_like(drop_wide)
    drop_wide[0:TR] = drop[...].astype(F32)
    live = jnp.sum(tok[...].astype(F32), axis=1, keepdims=True)

    def cell_mask(step):
        lane = lax.broadcasted_iota(jnp.int32, (1, WIDE), 1)
        tile_row = ((lane >> 6) & 1) * HALF + (lane >> 7) + 2 * step
        within = lane & 15
        tile_col = ((lane >> 4) & 3) * HALF + within
        grid_row = (tile_row + row * TR).astype(F32)
        grid_col = (tile_col + col * TC).astype(F32)
        one = jnp.where(grid_row < live, 1.0, 0.0) * jnp.where(grid_col < live, 1.0, 0.0)
        return one * jnp.where(within < HALF, 1.0, 0.0)

    def front(step, here, weights, keep, slope, flat):
        logits = dot(w_in_t[weights], stack[0:128, here])
        squash = jax.nn.sigmoid(logits[128:])
        masked = squash * cell_mask(step)
        values = logits[:128] * masked
        keep[:, here] = masked
        slope[:, here] = values * (1.0 - squash)
        scatter(flat, step, values)

    def front_a(step, here):
        cells = turned(result_cells, step)
        pair_t[:, here] = cells
        centered = cells - mean0(cells)
        root = lax.rsqrt(mean0(centered * centered) + LN_EPS)
        rough = centered * root
        hat[:, here] = rough
        scale[:, here] = root
        stack[0:128, here] = (rough * columns[0] + columns[1]).astype(BF16)
        stack[128:256, here] = rough.astype(BF16)
        front(step, here, slice(0, 256), keep_a, slope_a, flat_a)

    result_cells[...] = pair[...].astype(F32)
    each(front_a)
    send_a[...] = flat_a[...].astype(BF16)
    pl.semaphore_wait(barrier, DEVICES - 1)
    send(send_a, got_a, 0)
    each(lambda step, here: front(step, here, slice(256, 512), keep_b, slope_b, flat_b))
    send_b[...] = flat_b[...].astype(BF16)
    send(send_b, got_b, 1)

    def prepare(step, here):
        squash = jax.nn.sigmoid(dot(w_in_t[512:640], stack[0:128, here]))
        lane = lax.broadcasted_iota(jnp.int32, (32, WIDE), 1)
        chosen = ((lane >> 6) & 1) * HALF + (lane >> 7) + 2 * step
        pick = (lax.broadcasted_iota(jnp.int32, (32, WIDE), 0) == chosen).astype(BF16)
        bits = dot_tn(drop_wide[...].astype(BF16), pick)
        kept = bits * (1.0 / KEEP_RATE)
        upstream = turned(grad_cells, step)
        cot_t[:, here] = upstream
        lift_keep[:, here] = kept * squash
        pulled = upstream * kept * squash
        logit_keep[:, here] = pulled * (1.0 - squash)
        lifted_back = pulled.astype(BF16)
        d_lifted[:, here] = lifted_back
        grad_mixed[:, here] = dot(w_out[...], lifted_back)

    grad_cells[...] = cot[...].astype(F32)
    each(prepare)
    arrived(got_a, 0)
    assemble(got_a, left)
    arrived(got_b, 1)
    assemble(got_b, right)
    square[...] = dot_tn(left[...], right[...])
    split(square, send_p)
    send(send_p, got_p, 2)

    arrived(got_p, 2)
    flat_a[...] = got_p[...].astype(F32)

    def tail_back(step, here):
        cells = gather(flat_a, step)
        centered = cells - mean0(cells)
        root = lax.rsqrt(mean0(centered * centered) + LN_EPS)
        rough = centered * root
        mid_hat[:, here] = rough
        pulled = grad_mixed[:, here] * columns[2]
        scatter(flat_b, step, root * (pulled - mean0(pulled) - rough * mean0(pulled * rough)))

    each(tail_back)
    send_d[...] = flat_b[...].astype(BF16)
    send(send_d, got_d, 3)

    totals[...] = jnp.zeros_like(totals)

    def total(which, values):
        totals[which] += values[:, :128] + values[:, 128:]

    def tail_front(step, here):
        rough = mid_hat[:, here]
        blended = (rough * columns[2] + columns[3]).astype(BF16)
        mixed[:, here] = blended
        lifted = dot(w_out_t[...], blended)
        turn_back(result_cells, step, (pair_t[:, here] + lift_keep[:, here] * lifted).astype(BF16))
        logit = (logit_keep[:, here] * lifted).astype(BF16)
        d_all[512:640, here] = logit
        pulled = grad_mixed[:, here]
        total(2, pulled * rough)
        total(3, pulled)

    each(tail_front)
    pair[...] = result_cells[...].astype(BF16)
    hand_result = pltpu.make_async_copy(pair, result, local_sem.at[14])
    hand_result.start()
    sums_flat[...] = jnp.zeros_like(sums_flat)

    def put_sums(which, values):
        sums_flat[pl.ds(which, OWNERS, stride=PART), :] = values[:OWNERS]
        sums_flat[pl.ds(which + 6, OWNERS, stride=PART), :] = values[OWNERS:]

    def put_front(first, last):
        outer = dot_nt(stack[...], d_all[128 * first : 128 * last])
        for which in range(first, last):
            here = slice(128 * (which - first), 128 * (which - first) + 128)
            put_sums(which, outer[0:128, here])
            weight = w_all[:, 128 * which : 128 * which + 128].astype(F32)
            totals[0] += outer[128:256, here] * weight
            totals[1] += outer[256:257, here] * weight

    def put_vector(which):
        sums_flat[12 + which : 13 + which] = jnp.sum(totals[which].T, axis=0, keepdims=True)

    put_front(4, 5)
    put_sums(5, dot_nt(mixed[...], d_lifted[...]))
    put_vector(2)
    put_vector(3)

    arrived(got_d, 3)
    assemble(got_d, turn)
    square[...] = dot_nt(right[...], turn[...])
    split(square, send_ga)
    send(send_ga, got_ga, 4)
    square[...] = dot(left[...], turn[...])
    split(square, send_gb)
    send(send_gb, got_gb, 5)

    def front_back(first, flat, keep, slope):
        def run(step, here):
            cells = gather(flat, step)
            d_all[first : first + 128, here] = (cells * keep[:, here]).astype(BF16)
            d_all[first + 128 : first + 256, here] = (cells * slope[:, here]).astype(BF16)

        return run

    arrived(got_ga, 4)
    flat_a[...] = got_ga[...].astype(F32)
    each(front_back(0, flat_a, keep_a, slope_a))
    put_front(0, 2)
    arrived(got_gb, 5)
    flat_b[...] = got_gb[...].astype(F32)
    each(front_back(256, flat_b, keep_b, slope_b))
    put_front(2, 4)
    put_vector(0)
    put_vector(1)
    sums_send[...] = sums_flat[...].astype(BF16)

    chip = (row // 2) * COLS + col
    mine = pl.ds(pl.multiple_of(me * PART, PART), PART)
    owned = pl.ds(pl.multiple_of(chip * PART, PART), PART)

    def start_sum(x, y, z):
        home = part_x[x] + part_y[y] + part_z[z]
        owner = (home // 16) * COLS + lax.rem(home, COLS)
        pltpu.make_async_remote_copy(
            src_ref=sums_send.at[pl.ds(pl.multiple_of(owner * PART, PART), PART)],
            dst_ref=sums_got.at[mine],
            send_sem=send_sem.at[6],
            recv_sem=recv_sem.at[6],
            device_id=place(home),
            device_id_type=pl.DeviceIdType.MESH,
        ).start()

    for x, y, z, _ in partners(1):
        start_sum(x, y, z)

    @pl.when(core == 1)
    def _():
        start_sum(0, 0, 0)

    def finish(step, here):
        pulled = dot(w_all[...], d_all[:, here]) * columns[0]
        rough = hat[:, here]
        back = scale[:, here] * (pulled - mean0(pulled) - rough * mean0(pulled * rough))
        turn_back(grad_cells, step, (cot_t[:, here] + back).astype(BF16))

    each(finish)
    cot[...] = grad_cells[...].astype(BF16)
    hand_grad = pltpu.make_async_copy(cot, pair_grad, local_sem.at[15])
    hand_grad.start()

    @pl.when(core == 0)
    def _():
        sums_got[mine] = sums_send[owned]
        arrived(sums_got, 6)
        whole = jnp.sum(sums_got[...].astype(F32).reshape(DEVICES, PART, 128), axis=0)
        share[...] = (whole * (1.0 / TOKENS)).astype(BF16)

        for offset in partners(2):
            pltpu.make_async_remote_copy(
                src_ref=share,
                dst_ref=sums.at[owned],
                send_sem=send_sem.at[7],
                recv_sem=recv_sem.at[7],
                device_id=place(device_at(*offset)),
                device_id_type=pl.DeviceIdType.MESH,
            ).start()

        sums[owned] = share[...]
        settle(sums, recv_sem, 7, (OWNERS - 1) * PART)
        settle(sums_got, send_sem, 7, (DEVICES - 1) * PART)
        settle(sums_send, send_sem, 6, (OWNERS - 1) * PART)

    @pl.when(core == 1)
    def _():
        settle(sums, recv_sem, 7, OWNERS * PART)
        settle(sums_send, send_sem, 6, OWNERS * PART)

    hand_sums = pltpu.make_async_copy(sums, all_sums, local_sem.at[16])
    hand_sums.start()
    for slot, source in enumerate((send_a, send_b, send_p, send_d, send_ga, send_gb)):
        settle(source, send_sem, slot, (DEVICES - 1) * PART)
    for hand in (hand_result, hand_grad, hand_sums):
        hand.wait()


def hand_out(*refs):
    inputs, outputs, refs = refs[:3], refs[3:15], refs[15:]
    held, sums_flat, ready, sem = refs[:3], refs[3], refs[4:14], refs[14]
    fetches = [
        pltpu.make_async_copy(inputs[which], held[which], sem.at[which]) for which in range(3)
    ]
    hands = [
        pltpu.make_async_copy(held[which], outputs[which], sem.at[3 + which]) for which in range(2)
    ]
    hands += [
        pltpu.make_async_copy(ready[which], outputs[2 + which], sem.at[5 + which])
        for which in range(10)
    ]
    for which in (2, 0, 1):
        fetches[which].start()
    fetches[2].wait()
    sums_flat[...] = held[2][...].astype(F32)
    for which in range(6):
        ready[which][0:OWNERS] = sums_flat[pl.ds(which, OWNERS, stride=PART), :]
        ready[which][OWNERS:] = sums_flat[pl.ds(which + 6, OWNERS, stride=PART), :]
        hands[2 + which].start()
    for which in range(4):
        ready[6 + which][...] = sums_flat[12 + which : 13 + which]
        hands[8 + which].start()
    for which in range(2):
        fetches[which].wait()
        hands[which].start()
    for hand in hands:
        hand.wait()


def body(pair, cotangent, *rest):
    weights, vectors, drop_bits, tok_mask = rest[:6], rest[6:10], rest[10], rest[11]
    vmem = pltpu.VMEM
    block = vmem((DEVICES * PART, 128), BF16)
    blocks = [block] * 12
    squares = [vmem((SIDE, SIDE), BF16)] * 3 + [vmem((SIDE, SIDE), F32)]
    flats = [vmem((DEVICES * PART, 128), F32)] * 2
    half, full = vmem((128, CELLS), BF16), vmem((128, CELLS), F32)
    square, tile = vmem((128, 128), BF16), (TR * TC, 128)
    scratch = [vmem(tile, BF16)] * 2 + [square] * 6 + [vmem((1, 128), F32)] * 4
    scratch += [vmem((TR, 128), jnp.int32), vmem((1, TOKENS), jnp.int32)]
    scratch += [vmem(tile, F32)] * 2
    scratch += [vmem((2 * TC, 128), BF16), vmem((OWNERS * PART, 128), BF16)]
    scratch += blocks + squares + flats
    scratch += [vmem((128, 128), BF16), vmem((640, 128), BF16), vmem((128, 128), BF16)]
    scratch += [vmem((128, 640), BF16), vmem((4, 128, WIDE), F32), vmem((32, 128), F32)]
    scratch += [vmem((272, CELLS), BF16), full, vmem((1, CELLS), F32)] + [full] * 8
    scratch += [half, full, full, half, vmem((640, CELLS), BF16)]
    scratch += [vmem((4, 128, 128), F32), vmem((OWNERS * PART, 128), F32)]
    scratch += [vmem((OWNERS * PART, 128), BF16), block, vmem((PART, 128), BF16)]
    scratch += [pltpu.SemaphoreType.DMA((8,))] * 2 + [pltpu.SemaphoreType.DMA((17,))]
    anywhere = pl.BlockSpec(memory_space=pl.ANY)
    done = pl.pallas_call(
        kernel,
        out_shape=[
            jax.ShapeDtypeStruct(tile, BF16),
            jax.ShapeDtypeStruct(tile, BF16),
            jax.ShapeDtypeStruct((OWNERS * PART, 128), BF16),
        ],
        in_specs=[anywhere] * 14,
        out_specs=[anywhere] * 3,
        scratch_shapes=scratch,
        compiler_params=pltpu.CompilerParams(
            collective_id=0, has_side_effects=True, vmem_limit_bytes=60 * 2**20
        ),
    )(
        pair.reshape(tile),
        cotangent.reshape(tile),
        *weights,
        *(vector.reshape(1, 128) for vector in vectors),
        drop_bits,
        tok_mask.reshape(1, TOKENS),
    )
    outs = pl.pallas_call(
        hand_out,
        out_shape=[jax.ShapeDtypeStruct(tile, BF16)] * 2
        + [jax.ShapeDtypeStruct((128, 128), F32)] * 6
        + [jax.ShapeDtypeStruct((1, 128), F32)] * 4,
        in_specs=[anywhere] * 3,
        out_specs=[anywhere] * 12,
        scratch_shapes=[vmem(tile, BF16)] * 2
        + [vmem((OWNERS * PART, 128), BF16), vmem((OWNERS * PART, 128), F32)]
        + [vmem((128, 128), F32)] * 6
        + [vmem((1, 128), F32)] * 4
        + [pltpu.SemaphoreType.DMA((15,))],
        compiler_params=pltpu.CompilerParams(vmem_limit_bytes=60 * 2**20),
    )(*done)
    result, pair_grad = outs[0].reshape(TR, TC, 128), outs[1].reshape(TR, TC, 128)
    return (result, pair_grad) + tuple(outs[2:8]) + tuple(out.reshape(128) for out in outs[8:])


def solution(mesh):
    tiles = P("row", "col", None)
    return jax.shard_map(
        body,
        mesh=mesh,
        in_specs=(tiles, tiles) + (P(),) * 10 + (P("row", None), P()),
        out_specs=(tiles, tiles) + (P(),) * 10,
        check_vma=False,
    )
```

```python
import jax
import jax.numpy as jnp
from jax import lax
from jax.experimental import pallas as pl
from jax.experimental.pallas import tpu as pltpu
from jax.sharding import PartitionSpec as P

LN_EPS = 1e-05
KEEP_RATE = 0.75
ROWS, COLS = 16, 8
DEVICES = ROWS * COLS
TR, TC = 28, 56
TOKENS = 448
WIDE = 256
STEPS = 7
CELLS = WIDE * STEPS
SIDE = 512
PART = 16
HALF = 14
OWNERS = DEVICES // 2
BF16 = jnp.bfloat16
F32 = jnp.float32


def partners(cores):
    offsets = [
        (x, y, z, core)
        for x in range(4)
        for y in range(4)
        for z in range(4)
        for core in range(cores)
        if x or y or z or core
    ]

    def rank(offset):
        far = sum(min(step, 4 - step) for step in offset[:3])
        x, y, z, core = offset
        return -far, (29 * x + 13 * y + 7 * z + 17 * core) % 31, offset

    return sorted(offsets, key=rank)


def dot(left, right):
    return jnp.dot(left, right, preferred_element_type=F32)


def dot_nt(left, right):
    return lax.dot_general(left, right, (((1,), (1,)), ((), ())), preferred_element_type=F32)


def dot_tn(left, right):
    return lax.dot_general(left, right, (((0,), (0,)), ((), ())), preferred_element_type=F32)


def mean0(values):
    return jnp.mean(values, axis=0, keepdims=True)


def swap_halves(first, second):
    low = lax.broadcasted_iota(jnp.int32, first.shape, 1) < 64
    turned_first = pltpu.roll(first, 64, 1)
    turned_second = pltpu.roll(second, 64, 1)
    return jnp.where(low, first, turned_second), jnp.where(low, turned_first, second)


def kernel(*refs):
    inputs, refs = refs[:14], refs[14:]
    outputs, refs = refs[:3], refs[3:]
    run_kernel(inputs, outputs, refs[:14], *refs[14:])


def run_kernel(
    inputs,
    outputs,
    local,
    result_cells,
    grad_cells,
    pick_cells,
    sums,
    send_a,
    send_b,
    send_p,
    send_d,
    send_ga,
    send_gb,
    got_a,
    got_b,
    got_p,
    got_d,
    got_ga,
    got_gb,
    left,
    left_t,
    right,
    turn,
    square,
    flat_a,
    flat_b,
    eye,
    w_in_t,
    w_out_t,
    w_all,
    columns,
    drop_wide,
    stack,
    hat,
    scale,
    keep_a,
    slope_a,
    keep_b,
    slope_b,
    pair_t,
    cot_t,
    lift_keep,
    logit_keep,
    d_lifted,
    grad_mixed,
    centered_mixed,
    mid_hat,
    mixed,
    d_all,
    totals,
    sums_flat,
    sums_send,
    sums_got,
    share,
    send_sem,
    recv_sem,
    local_sem,
):
    result, pair_grad, all_sums = outputs
    pair, cot, w_a_proj, w_a_gate, w_b_proj, w_b_gate, w_gate, w_out = local[:8]
    in_gain, in_bias, mid_gain, mid_bias, drop, tok = local[8:]
    fetches = [
        pltpu.make_async_copy(inputs[which], local[which], local_sem.at[which])
        for which in range(14)
    ]
    for fetch in fetches:
        fetch.start()
    row, col = lax.axis_index("row"), lax.axis_index("col")
    me = row * COLS + col
    barrier = pltpu.get_barrier_semaphore()

    def place(peer):
        return (peer // COLS, lax.rem(peer, COLS))

    core = lax.rem(row, 2)
    at_x, at_y, at_z = lax.rem(row // 2, 2) * 2 + col // 4, row // 4, lax.rem(col, 4)
    steps_x = [lax.rem(at_x + step, 4) for step in range(4)]
    part_x = [(step // 2) * 16 + lax.rem(step, 2) * 4 for step in steps_x]
    part_y = [lax.rem(at_y + step, 4) * 32 for step in range(4)]
    part_z = [lax.rem(at_z + step, 4) for step in range(4)]
    part_core = [lax.rem(core + step, 2) * 8 for step in range(2)]

    def device_at(x, y, z, other_core):
        return part_x[x] + part_y[y] + part_z[z] + part_core[other_core]

    for offset in partners(2):
        pl.semaphore_signal(
            barrier,
            inc=1,
            device_id=place(device_at(*offset)),
            device_id_type=pl.DeviceIdType.MESH,
        )

    def send(source, target, slot, size=PART):
        mine = pl.ds(pl.multiple_of(me * size, size), size)

        for offset in partners(2):
            peer = device_at(*offset)
            pltpu.make_async_remote_copy(
                src_ref=source.at[pl.ds(pl.multiple_of(peer * size, size), size)],
                dst_ref=target.at[mine],
                send_sem=send_sem.at[slot],
                recv_sem=recv_sem.at[slot],
                device_id=place(peer),
                device_id_type=pl.DeviceIdType.MESH,
            ).start()
        target[mine] = source[mine]

    def settle(ref, sem, slot, length):
        some = ref.at[pl.ds(0, length)]
        pltpu.make_async_copy(some, some, sem.at[slot]).wait()

    def arrived(target, slot, size=PART):
        settle(target, recv_sem, slot, (DEVICES - 1) * size)

    def lanes(step):
        return pl.ds(pl.multiple_of(step * WIDE, WIDE), WIDE)

    def each(body):
        def run(step, carry):
            body(step, lanes(step))
            return carry

        lax.fori_loop(0, STEPS, run, 0, unroll=STEPS)

    def scatter(flat, step, values, stride=PART, shift=0):
        flat[pl.ds(2 * step + shift, 128, stride=stride), :] = values[:, :128]
        flat[pl.ds(2 * step + shift + 1, 128, stride=stride), :] = values[:, 128:]

    def gather(flat, step):
        return jnp.concatenate(
            [
                flat[pl.ds(2 * step, 128, stride=PART), :],
                flat[pl.ds(2 * step + 1, 128, stride=PART), :],
            ],
            axis=1,
        )

    def tile_rows(step, part):
        first = pl.multiple_of((2 * step + part) * TC, 8)
        second = pl.multiple_of((2 * step + part + HALF) * TC, 8)
        return pl.ds(first, TC), pl.ds(second, TC)

    def turned(ref, step):
        parts = []
        for part in range(2):
            first, second = tile_rows(step, part)
            cells = jnp.concatenate([ref[first], ref[second]], axis=0).astype(BF16)
            parts.append(dot_tn(cells, pick_cells[...]))
        return jnp.concatenate(parts, axis=1)

    def turn_back(ref, step, values):
        for part in range(2):
            first, second = tile_rows(step, part)
            cells = dot_nt(pick_cells[...], values[:, 128 * part : 128 * part + 128])
            ref[first] = cells[:TC]
            ref[second] = cells[TC:]

    def assemble(blocks, matrix, stride=PART, shift=0):
        def run(index, carry):
            base = pl.multiple_of(index * COLS * stride, COLS * stride)
            top = pl.multiple_of(index * 32, 32)
            for pick in range(4):
                one = blocks[pl.ds(base + 2 * pick * stride + shift, PART)].astype(F32)
                two = blocks[pl.ds(base + (2 * pick + 1) * stride + shift, PART)].astype(F32)
                upper, lower = swap_halves(one, two)
                here = pl.ds(128 * pick, 128)
                matrix[pl.ds(top, PART), here] = upper.astype(BF16)
                matrix[pl.ds(top + PART, PART), here] = lower.astype(BF16)
            return carry

        lax.fori_loop(0, ROWS, run, 0, unroll=ROWS)

    def split(matrix, blocks):
        def run(index, carry):
            base = pl.multiple_of(index * 128, 128)
            top = pl.multiple_of(index * 32, 32)
            for pick in range(4):
                here = pl.ds(128 * pick, 128)
                upper = matrix[pl.ds(top, PART), here]
                lower = matrix[pl.ds(top + PART, PART), here]
                one, two = swap_halves(upper, lower)
                blocks[pl.ds(base + 32 * pick, PART)] = one.astype(BF16)
                blocks[pl.ds(base + 32 * pick + PART, PART)] = two.astype(BF16)
            return carry

        lax.fori_loop(0, ROWS, run, 0, unroll=ROWS)

    for spare in range(HALF, PART):
        flat_a[pl.ds(spare, 128, stride=PART), :] = jnp.zeros((128, 128), F32)
        flat_b[pl.ds(spare, 128, stride=PART), :] = jnp.zeros((128, 128), F32)
    eye[...] = (
        lax.broadcasted_iota(jnp.int32, (128, 128), 0)
        == lax.broadcasted_iota(jnp.int32, (128, 128), 1)
    ).astype(BF16)
    lane = lax.broadcasted_iota(jnp.int32, (2 * TC, 128), 1)
    wanted = (lane >> 6) * TC + ((lane >> 4) & 3) * HALF + (lane & 15)
    chosen_cell = lax.broadcasted_iota(jnp.int32, (2 * TC, 128), 0) == wanted
    chosen_cell = jnp.where(chosen_cell, 1.0, 0.0) * jnp.where((lane & 15) < HALF, 1.0, 0.0)
    pick_cells[...] = chosen_cell.astype(BF16)
    for fetch in fetches:
        fetch.wait()
    def put_weight(which, weight):
        here = slice(128 * which, 128 * which + 128)
        w_in_t[here] = dot_nt(eye[...], weight[...]).astype(BF16)
        w_all[:, here] = weight[...]

    def put_column(which, vector):
        column = jnp.broadcast_to(vector[...], (128, 128)).T
        columns[which] = jnp.concatenate([column, column], axis=1)

    put_weight(0, w_a_proj)
    put_weight(1, w_a_gate)
    put_column(0, in_gain)
    put_column(1, in_bias)
    live = jnp.sum(tok[...].astype(F32), axis=1, keepdims=True)

    def cell_mask(step):
        lane = lax.broadcasted_iota(jnp.int32, (1, WIDE), 1)
        tile_row = ((lane >> 6) & 1) * HALF + (lane >> 7) + 2 * step
        within = lane & 15
        tile_col = ((lane >> 4) & 3) * HALF + within
        grid_row = (tile_row + row * TR).astype(F32)
        grid_col = (tile_col + col * TC).astype(F32)
        one = jnp.where(grid_row < live, 1.0, 0.0) * jnp.where(grid_col < live, 1.0, 0.0)
        return one * jnp.where(within < HALF, 1.0, 0.0)

    def front(step, here, weights, keep, slope, flat):
        logits = dot(w_in_t[weights], stack[0:128, here])
        squash = jax.nn.sigmoid(logits[128:])
        masked = squash * cell_mask(step)
        values = logits[:128] * masked
        keep[:, here] = masked
        slope[:, here] = values * (1.0 - squash)
        scatter(flat, step, values)

    def front_a(step, here):
        cells = turned(result_cells, step)
        pair_t[:, here] = cells
        centered = cells - mean0(cells)
        root = lax.rsqrt(mean0(centered * centered) + LN_EPS)
        rough = centered * root
        hat[:, here] = rough
        scale[:, here] = root
        stack[0:128, here] = (rough * columns[0] + columns[1]).astype(BF16)
        stack[128:256, here] = rough.astype(BF16)
        front(step, here, slice(0, 256), keep_a, slope_a, flat_a)

    result_cells[...] = pair[...].astype(F32)
    each(front_a)
    send_a[...] = flat_a[...].astype(BF16)
    pl.semaphore_wait(barrier, DEVICES - 1)
    send(send_a, got_a, 0)
    put_weight(2, w_b_proj)
    put_weight(3, w_b_gate)
    each(lambda step, here: front(step, here, slice(256, 512), keep_b, slope_b, flat_b))
    send_b[...] = flat_b[...].astype(BF16)
    send(send_b, got_b, 1)
    put_weight(4, w_gate)
    w_out_t[...] = dot_nt(eye[...], w_out[...]).astype(BF16)
    put_column(2, mid_gain)
    put_column(3, mid_bias)
    stack[256:272] = jnp.ones((16, CELLS), BF16)
    drop_wide[...] = jnp.zeros_like(drop_wide)
    drop_wide[0:TR] = drop[...].astype(F32)

    def prepare(step, here):
        squash = jax.nn.sigmoid(dot(w_in_t[512:640], stack[0:128, here]))
        lane = lax.broadcasted_iota(jnp.int32, (32, WIDE), 1)
        chosen = ((lane >> 6) & 1) * HALF + (lane >> 7) + 2 * step
        pick = (lax.broadcasted_iota(jnp.int32, (32, WIDE), 0) == chosen).astype(BF16)
        bits = dot_tn(drop_wide[...].astype(BF16), pick)
        kept = bits * (1.0 / KEEP_RATE)
        upstream = turned(grad_cells, step)
        cot_t[:, here] = upstream
        lift_keep[:, here] = kept * squash
        pulled = upstream * kept * squash
        logit_keep[:, here] = pulled * (1.0 - squash)
        lifted_back = pulled.astype(BF16)
        d_lifted[:, here] = lifted_back
        pulled_mixed = dot(w_out[...], lifted_back)
        grad_mixed[:, here] = pulled_mixed
        scaled = pulled_mixed * columns[2]
        centered_mixed[:, here] = scaled - mean0(scaled)

    grad_cells[...] = cot[...].astype(F32)
    each(prepare)
    arrived(got_a, 0)
    assemble(got_a, left)
    for block in range(4):
        here = slice(128 * block, 128 * block + 128)
        left_t[here] = dot_nt(eye[...], left[:, here]).astype(BF16)
    arrived(got_b, 1)
    assemble(got_b, right)
    square[...] = dot(left_t[...], right[...])
    split(square, send_p)
    send(send_p, got_p, 2)

    arrived(got_p, 2)
    flat_a[...] = got_p[...].astype(F32)

    def tail_back(step, here):
        cells = gather(flat_a, step)
        centered = cells - mean0(cells)
        root = lax.rsqrt(mean0(centered * centered) + LN_EPS)
        rough = centered * root
        mid_hat[:, here] = rough
        pulled = centered_mixed[:, here]
        scatter(flat_b, step, root * (pulled - rough * mean0(pulled * rough)))

    each(tail_back)
    send_d[...] = flat_b[...].astype(BF16)
    send(send_d, got_d, 3)

    totals[...] = jnp.zeros_like(totals)

    def total(which, values):
        totals[which] += values[:, :128] + values[:, 128:]

    def tail_front(step, here):
        rough = mid_hat[:, here]
        blended = (rough * columns[2] + columns[3]).astype(BF16)
        mixed[:, here] = blended
        lifted = dot(w_out_t[...], blended)
        turn_back(result_cells, step, (pair_t[:, here] + lift_keep[:, here] * lifted).astype(BF16))
        logit = (logit_keep[:, here] * lifted).astype(BF16)
        d_all[512:640, here] = logit
        pulled = grad_mixed[:, here]
        total(2, pulled * rough)
        total(3, pulled)

    each(tail_front)
    pair[...] = result_cells[...].astype(BF16)
    hand_result = pltpu.make_async_copy(pair, result, local_sem.at[14])
    hand_result.start()
    sums_flat[...] = jnp.zeros_like(sums_flat)

    def put_sums(which, values):
        sums_flat[pl.ds(which, OWNERS, stride=PART), :] = values[:OWNERS]
        sums_flat[pl.ds(which + 6, OWNERS, stride=PART), :] = values[OWNERS:]

    def put_front(first, last):
        outer = dot_nt(stack[...], d_all[128 * first : 128 * last])
        for which in range(first, last):
            here = slice(128 * (which - first), 128 * (which - first) + 128)
            put_sums(which, outer[0:128, here])
            weight = w_all[:, 128 * which : 128 * which + 128].astype(F32)
            totals[0] += outer[128:256, here] * weight
            totals[1] += outer[256:257, here] * weight

    def put_vector(which):
        sums_flat[12 + which : 13 + which] = jnp.sum(totals[which].T, axis=0, keepdims=True)

    put_front(4, 5)
    put_sums(5, dot_nt(mixed[...], d_lifted[...]))
    put_vector(2)
    put_vector(3)

    arrived(got_d, 3)
    assemble(got_d, turn)
    square[...] = dot_nt(right[...], turn[...])
    split(square, send_ga)
    send(send_ga, got_ga, 4)
    square[...] = dot(left[...], turn[...])
    split(square, send_gb)
    send(send_gb, got_gb, 5)

    def front_back(first, flat, keep, slope):
        def run(step, here):
            cells = gather(flat, step)
            d_all[first : first + 128, here] = (cells * keep[:, here]).astype(BF16)
            d_all[first + 128 : first + 256, here] = (cells * slope[:, here]).astype(BF16)

        return run

    arrived(got_ga, 4)
    flat_a[...] = got_ga[...].astype(F32)
    each(front_back(0, flat_a, keep_a, slope_a))
    put_front(0, 2)
    arrived(got_gb, 5)
    flat_b[...] = got_gb[...].astype(F32)
    each(front_back(256, flat_b, keep_b, slope_b))
    put_front(2, 4)
    put_vector(0)
    put_vector(1)
    sums_send[...] = sums_flat[...].astype(BF16)

    chip = (row // 2) * COLS + col
    mine = pl.ds(pl.multiple_of(me * PART, PART), PART)
    owned = pl.ds(pl.multiple_of(chip * PART, PART), PART)

    def start_sum(x, y, z):
        home = part_x[x] + part_y[y] + part_z[z]
        owner = (home // 16) * COLS + lax.rem(home, COLS)
        pltpu.make_async_remote_copy(
            src_ref=sums_send.at[pl.ds(pl.multiple_of(owner * PART, PART), PART)],
            dst_ref=sums_got.at[mine],
            send_sem=send_sem.at[6],
            recv_sem=recv_sem.at[6],
            device_id=place(home),
            device_id_type=pl.DeviceIdType.MESH,
        ).start()

    for x, y, z, _ in partners(1):
        start_sum(x, y, z)

    @pl.when(core == 1)
    def _():
        start_sum(0, 0, 0)

    def finish(step, here):
        pulled = dot(w_all[...], d_all[:, here]) * columns[0]
        rough = hat[:, here]
        back = scale[:, here] * (pulled - mean0(pulled) - rough * mean0(pulled * rough))
        turn_back(grad_cells, step, (cot_t[:, here] + back).astype(BF16))

    each(finish)
    cot[...] = grad_cells[...].astype(BF16)
    hand_grad = pltpu.make_async_copy(cot, pair_grad, local_sem.at[15])
    hand_grad.start()

    @pl.when(core == 0)
    def _():
        sums_got[mine] = sums_send[owned]
        arrived(sums_got, 6)
        whole = jnp.sum(sums_got[...].astype(F32).reshape(DEVICES, PART, 128), axis=0)
        share[...] = (whole * (1.0 / TOKENS)).astype(BF16)

        for offset in partners(2):
            pltpu.make_async_remote_copy(
                src_ref=share,
                dst_ref=sums.at[owned],
                send_sem=send_sem.at[7],
                recv_sem=recv_sem.at[7],
                device_id=place(device_at(*offset)),
                device_id_type=pl.DeviceIdType.MESH,
            ).start()

        sums[owned] = share[...]
        settle(sums, recv_sem, 7, (OWNERS - 1) * PART)
        settle(sums_got, send_sem, 7, (DEVICES - 1) * PART)
        settle(sums_send, send_sem, 6, (OWNERS - 1) * PART)

    @pl.when(core == 1)
    def _():
        settle(sums, recv_sem, 7, OWNERS * PART)
        settle(sums_send, send_sem, 6, OWNERS * PART)

    hand_sums = pltpu.make_async_copy(sums, all_sums, local_sem.at[16])
    hand_sums.start()
    for slot, source in enumerate((send_a, send_b, send_p, send_d, send_ga, send_gb)):
        settle(source, send_sem, slot, (DEVICES - 1) * PART)
    for hand in (hand_result, hand_grad, hand_sums):
        hand.wait()


def hand_out(*refs):
    inputs, outputs, refs = refs[:3], refs[3:15], refs[15:]
    held, sums_flat, ready, sem = refs[:3], refs[3], refs[4:14], refs[14]
    fetches = [
        pltpu.make_async_copy(inputs[which], held[which], sem.at[which]) for which in range(3)
    ]
    hands = [
        pltpu.make_async_copy(held[which], outputs[which], sem.at[3 + which]) for which in range(2)
    ]
    hands += [
        pltpu.make_async_copy(ready[which], outputs[2 + which], sem.at[5 + which])
        for which in range(10)
    ]
    for which in (2, 0, 1):
        fetches[which].start()
    fetches[2].wait()
    sums_flat[...] = held[2][...].astype(F32)
    for which in range(6):
        ready[which][0:OWNERS] = sums_flat[pl.ds(which, OWNERS, stride=PART), :]
        ready[which][OWNERS:] = sums_flat[pl.ds(which + 6, OWNERS, stride=PART), :]
        hands[2 + which].start()
    for which in range(4):
        ready[6 + which][...] = sums_flat[12 + which : 13 + which]
        hands[8 + which].start()
    for which in range(2):
        fetches[which].wait()
        hands[which].start()
    for hand in hands:
        hand.wait()


def body(pair, cotangent, *rest):
    weights, vectors, drop_bits, tok_mask = rest[:6], rest[6:10], rest[10], rest[11]
    vmem = pltpu.VMEM
    block = vmem((DEVICES * PART, 128), BF16)
    blocks = [block] * 12
    squares = [vmem((SIDE, SIDE), BF16)] * 4 + [vmem((SIDE, SIDE), F32)]
    flats = [vmem((DEVICES * PART, 128), F32)] * 2
    half, full = vmem((128, CELLS), BF16), vmem((128, CELLS), F32)
    square, tile = vmem((128, 128), BF16), (TR * TC, 128)
    scratch = [vmem(tile, BF16)] * 2 + [square] * 6 + [vmem((1, 128), F32)] * 4
    scratch += [vmem((TR, 128), jnp.int32), vmem((1, TOKENS), jnp.int32)]
    scratch += [vmem(tile, F32)] * 2
    scratch += [vmem((2 * TC, 128), BF16), vmem((OWNERS * PART, 128), BF16)]
    scratch += blocks + squares + flats
    scratch += [vmem((128, 128), BF16), vmem((640, 128), BF16), vmem((128, 128), BF16)]
    scratch += [vmem((128, 640), BF16), vmem((4, 128, WIDE), F32), vmem((32, 128), F32)]
    scratch += [vmem((272, CELLS), BF16), full, vmem((1, CELLS), F32)] + [full] * 8
    scratch += [half, full, full, full, half, vmem((640, CELLS), BF16)]
    scratch += [vmem((4, 128, 128), F32), vmem((OWNERS * PART, 128), F32)]
    scratch += [vmem((OWNERS * PART, 128), BF16), block, vmem((PART, 128), BF16)]
    scratch += [pltpu.SemaphoreType.DMA((8,))] * 2 + [pltpu.SemaphoreType.DMA((17,))]
    anywhere = pl.BlockSpec(memory_space=pl.ANY)
    done = pl.pallas_call(
        kernel,
        out_shape=[
            jax.ShapeDtypeStruct(tile, BF16),
            jax.ShapeDtypeStruct(tile, BF16),
            jax.ShapeDtypeStruct((OWNERS * PART, 128), BF16),
        ],
        in_specs=[anywhere] * 14,
        out_specs=[anywhere] * 3,
        scratch_shapes=scratch,
        compiler_params=pltpu.CompilerParams(
            collective_id=0, has_side_effects=True, vmem_limit_bytes=60 * 2**20
        ),
    )(
        pair.reshape(tile),
        cotangent.reshape(tile),
        *weights,
        *(vector.reshape(1, 128) for vector in vectors),
        drop_bits,
        tok_mask.reshape(1, TOKENS),
    )
    outs = pl.pallas_call(
        hand_out,
        out_shape=[jax.ShapeDtypeStruct(tile, BF16)] * 2
        + [jax.ShapeDtypeStruct((128, 128), F32)] * 6
        + [jax.ShapeDtypeStruct((1, 128), F32)] * 4,
        in_specs=[anywhere] * 3,
        out_specs=[anywhere] * 12,
        scratch_shapes=[vmem(tile, BF16)] * 2
        + [vmem((OWNERS * PART, 128), BF16), vmem((OWNERS * PART, 128), F32)]
        + [vmem((128, 128), F32)] * 6
        + [vmem((1, 128), F32)] * 4
        + [pltpu.SemaphoreType.DMA((15,))],
        compiler_params=pltpu.CompilerParams(vmem_limit_bytes=60 * 2**20),
    )(*done)
    result, pair_grad = outs[0].reshape(TR, TC, 128), outs[1].reshape(TR, TC, 128)
    return (result, pair_grad) + tuple(outs[2:8]) + tuple(out.reshape(128) for out in outs[8:])


def solution(mesh):
    tiles = P("row", "col", None)
    return jax.shard_map(
        body,
        mesh=mesh,
        in_specs=(tiles, tiles) + (P(),) * 10 + (P("row", None), P()),
        out_specs=(tiles, tiles) + (P(),) * 10,
        check_vma=False,
    )
```

```python
import jax
import jax.numpy as jnp
from jax import lax
from jax.experimental import pallas as pl
from jax.experimental.pallas import tpu as pltpu
from jax.sharding import PartitionSpec as P

LN_EPS = 1e-05
KEEP_RATE = 0.75
ROWS, COLS = 16, 8
DEVICES = ROWS * COLS
TR, TC = 28, 56
TOKENS = 448
WIDE = 256
STEPS = 7
CELLS = WIDE * STEPS
SIDE = 512
PART = 16
HALF = 14
BLOCK = DEVICES * PART
OWNERS = DEVICES // 2
SHARES = OWNERS * PART
BF16 = jnp.bfloat16
F32 = jnp.float32


def partners(cores):
    offsets = [
        (x, y, z, core)
        for x in range(4)
        for y in range(4)
        for z in range(4)
        for core in range(cores)
        if x or y or z or core
    ]

    def rank(offset):
        far = sum(min(step, 4 - step) for step in offset[:3])
        x, y, z, core = offset
        return -far, (29 * x + 13 * y + 7 * z + 17 * core) % 31, offset

    return sorted(offsets, key=rank)


def dot(left, right):
    return jnp.dot(left, right, preferred_element_type=F32)


def dot_nt(left, right):
    return lax.dot_general(left, right, (((1,), (1,)), ((), ())), preferred_element_type=F32)


def dot_tn(left, right):
    return lax.dot_general(left, right, (((0,), (0,)), ((), ())), preferred_element_type=F32)


def mean0(values):
    return jnp.mean(values, axis=0, keepdims=True)


def swap_halves(first, second):
    low = lax.broadcasted_iota(jnp.int32, first.shape, 1) < 64
    turned_first = pltpu.roll(first, 64, 1)
    turned_second = pltpu.roll(second, 64, 1)
    return jnp.where(low, first, turned_second), jnp.where(low, turned_first, second)


def kernel(*refs):
    inputs, refs = refs[:14], refs[14:]
    outputs, refs = refs[:3], refs[3:]
    run_kernel(inputs, outputs, refs[:14], *refs[14:])


def run_kernel(
    inputs,
    outputs,
    local,
    result_cells,
    grad_cells,
    pick_cells,
    sums,
    send_a,
    send_b,
    send_p,
    send_d,
    send_ga,
    send_gb,
    got_a,
    got_b,
    got_p,
    got_d,
    got_ga,
    got_gb,
    left,
    left_t,
    right,
    turn,
    square,
    flat_a,
    flat_b,
    eye,
    w_in_t,
    w_out_t,
    w_all,
    columns,
    drop_wide,
    stack,
    hat,
    scale,
    keep_a,
    slope_a,
    keep_b,
    slope_b,
    pair_t,
    cot_t,
    lift_keep,
    logit_keep,
    d_lifted,
    grad_mixed,
    centered_mixed,
    mid_hat,
    mixed,
    d_all,
    totals,
    sums_flat,
    sums_send,
    sums_got,
    share,
    send_sem,
    recv_sem,
    local_sem,
):
    result, pair_grad, all_sums = outputs
    pair, cot, w_a_proj, w_a_gate, w_b_proj, w_b_gate, w_gate, w_out = local[:8]
    in_gain, in_bias, mid_gain, mid_bias, drop, tok = local[8:]
    fetches = [
        pltpu.make_async_copy(inputs[which], local[which], local_sem.at[which])
        for which in range(14)
    ]
    for fetch in fetches:
        fetch.start()
    row, col = lax.axis_index("row"), lax.axis_index("col")
    me = row * COLS + col
    barrier = pltpu.get_barrier_semaphore()

    def place(peer):
        return (peer // COLS, lax.rem(peer, COLS))

    core = lax.rem(row, 2)
    at_x, at_y, at_z = lax.rem(row // 2, 2) * 2 + col // 4, row // 4, lax.rem(col, 4)
    steps_x = [lax.rem(at_x + step, 4) for step in range(4)]
    part_x = [(step // 2) * 16 + lax.rem(step, 2) * 4 for step in steps_x]
    part_y = [lax.rem(at_y + step, 4) * 32 for step in range(4)]
    part_z = [lax.rem(at_z + step, 4) for step in range(4)]
    part_core = [lax.rem(core + step, 2) * 8 for step in range(2)]

    def device_at(x, y, z, other_core):
        return part_x[x] + part_y[y] + part_z[z] + part_core[other_core]

    for offset in partners(2):
        pl.semaphore_signal(
            barrier,
            inc=1,
            device_id=place(device_at(*offset)),
            device_id_type=pl.DeviceIdType.MESH,
        )

    def send(source, target, slot, size=PART):
        mine = pl.ds(pl.multiple_of(me * size, size), size)

        for offset in partners(2):
            peer = device_at(*offset)
            pltpu.make_async_remote_copy(
                src_ref=source.at[pl.ds(pl.multiple_of(peer * size, size), size)],
                dst_ref=target.at[mine],
                send_sem=send_sem.at[slot],
                recv_sem=recv_sem.at[slot],
                device_id=place(peer),
                device_id_type=pl.DeviceIdType.MESH,
            ).start()
        target[mine] = source[mine]

    def settle(ref, sem, slot, length):
        some = ref.at[pl.ds(0, length)]
        pltpu.make_async_copy(some, some, sem.at[slot]).wait()

    def arrived(target, slot, size=PART):
        settle(target, recv_sem, slot, (DEVICES - 1) * size)

    def lanes(step):
        return pl.ds(pl.multiple_of(step * WIDE, WIDE), WIDE)

    def each(body):
        def run(step, carry):
            body(step, lanes(step))
            return carry

        lax.fori_loop(0, STEPS, run, 0, unroll=STEPS)

    def scatter(flat, step, values, stride=PART, shift=0):
        flat[pl.ds(2 * step + shift, 128, stride=stride), :] = values[:, :128]
        flat[pl.ds(2 * step + shift + 1, 128, stride=stride), :] = values[:, 128:]

    def gather(flat, step):
        return jnp.concatenate(
            [
                flat[pl.ds(2 * step, 128, stride=PART), :],
                flat[pl.ds(2 * step + 1, 128, stride=PART), :],
            ],
            axis=1,
        )

    def tile_rows(step, part):
        first = pl.multiple_of((2 * step + part) * TC, 8)
        second = pl.multiple_of((2 * step + part + HALF) * TC, 8)
        return pl.ds(first, TC), pl.ds(second, TC)

    def turned(ref, step):
        parts = []
        for part in range(2):
            first, second = tile_rows(step, part)
            cells = jnp.concatenate([ref[first], ref[second]], axis=0).astype(BF16)
            parts.append(dot_tn(cells, pick_cells[...]))
        return jnp.concatenate(parts, axis=1)

    def turn_back(ref, step, values):
        for part in range(2):
            first, second = tile_rows(step, part)
            cells = dot_nt(pick_cells[...], values[:, 128 * part : 128 * part + 128])
            ref[first] = cells[:TC]
            ref[second] = cells[TC:]

    def assemble(blocks, matrix, stride=PART, shift=0):
        def run(index, carry):
            base = pl.multiple_of(index * COLS * stride, COLS * stride)
            top = pl.multiple_of(index * 32, 32)
            for pick in range(4):
                one = blocks[pl.ds(base + 2 * pick * stride + shift, PART)].astype(F32)
                two = blocks[pl.ds(base + (2 * pick + 1) * stride + shift, PART)].astype(F32)
                upper, lower = swap_halves(one, two)
                here = pl.ds(128 * pick, 128)
                matrix[pl.ds(top, PART), here] = upper.astype(BF16)
                matrix[pl.ds(top + PART, PART), here] = lower.astype(BF16)
            return carry

        lax.fori_loop(0, ROWS, run, 0, unroll=ROWS)

    def split(matrix, blocks):
        def run(index, carry):
            base = pl.multiple_of(index * 128, 128)
            top = pl.multiple_of(index * 32, 32)
            for pick in range(4):
                here = pl.ds(128 * pick, 128)
                upper = matrix[pl.ds(top, PART), here]
                lower = matrix[pl.ds(top + PART, PART), here]
                one, two = swap_halves(upper, lower)
                blocks[pl.ds(base + 32 * pick, PART)] = one.astype(BF16)
                blocks[pl.ds(base + 32 * pick + PART, PART)] = two.astype(BF16)
            return carry

        lax.fori_loop(0, ROWS, run, 0, unroll=ROWS)

    for spare in range(HALF, PART):
        flat_a[pl.ds(spare, 128, stride=PART), :] = jnp.zeros((128, 128), F32)
        flat_b[pl.ds(spare, 128, stride=PART), :] = jnp.zeros((128, 128), F32)
    eye[...] = (
        lax.broadcasted_iota(jnp.int32, (128, 128), 0)
        == lax.broadcasted_iota(jnp.int32, (128, 128), 1)
    ).astype(BF16)
    lane = lax.broadcasted_iota(jnp.int32, (2 * TC, 128), 1)
    wanted = (lane >> 6) * TC + ((lane >> 4) & 3) * HALF + (lane & 15)
    chosen_cell = lax.broadcasted_iota(jnp.int32, (2 * TC, 128), 0) == wanted
    chosen_cell = jnp.where(chosen_cell, 1.0, 0.0) * jnp.where((lane & 15) < HALF, 1.0, 0.0)
    pick_cells[...] = chosen_cell.astype(BF16)
    for fetch in fetches:
        fetch.wait()
    def put_weight(which, weight):
        here = slice(128 * which, 128 * which + 128)
        w_in_t[here] = dot_nt(eye[...], weight[...]).astype(BF16)
        w_all[:, here] = weight[...]

    def put_column(which, vector):
        column = jnp.broadcast_to(vector[...], (128, 128)).T
        columns[which] = jnp.concatenate([column, column], axis=1)

    put_weight(0, w_a_proj)
    put_weight(1, w_a_gate)
    put_column(0, in_gain)
    put_column(1, in_bias)
    live = jnp.sum(tok[...].astype(F32), axis=1, keepdims=True)

    def cell_mask(step):
        lane = lax.broadcasted_iota(jnp.int32, (1, WIDE), 1)
        tile_row = ((lane >> 6) & 1) * HALF + (lane >> 7) + 2 * step
        within = lane & 15
        tile_col = ((lane >> 4) & 3) * HALF + within
        grid_row = (tile_row + row * TR).astype(F32)
        grid_col = (tile_col + col * TC).astype(F32)
        one = jnp.where(grid_row < live, 1.0, 0.0) * jnp.where(grid_col < live, 1.0, 0.0)
        return one * jnp.where(within < HALF, 1.0, 0.0)

    def front(step, here, weights, keep, slope, flat):
        logits = dot(w_in_t[weights], stack[0:128, here])
        squash = jax.nn.sigmoid(logits[128:])
        masked = squash * cell_mask(step)
        values = logits[:128] * masked
        keep[:, here] = masked
        slope[:, here] = values * (1.0 - squash)
        scatter(flat, step, values)

    def front_a(step, here):
        cells = turned(result_cells, step)
        pair_t[:, here] = cells
        centered = cells - mean0(cells)
        root = lax.rsqrt(mean0(centered * centered) + LN_EPS)
        rough = centered * root
        hat[:, here] = rough
        scale[:, here] = root
        stack[0:128, here] = (rough * columns[0] + columns[1]).astype(BF16)
        stack[128:256, here] = rough.astype(BF16)
        front(step, here, slice(0, 256), keep_a, slope_a, flat_a)

    result_cells[...] = pair[...].astype(F32)
    each(front_a)
    send_a[...] = flat_a[0:BLOCK].astype(BF16)
    pl.semaphore_wait(barrier, DEVICES - 1)
    send(send_a, got_a, 0)
    put_weight(2, w_b_proj)
    put_weight(3, w_b_gate)
    each(lambda step, here: front(step, here, slice(256, 512), keep_b, slope_b, flat_b))
    send_b[...] = flat_b[0:BLOCK].astype(BF16)
    send(send_b, got_b, 1)
    put_weight(4, w_gate)
    w_out_t[...] = dot_nt(eye[...], w_out[...]).astype(BF16)
    put_column(2, mid_gain)
    put_column(3, mid_bias)
    stack[256:272] = jnp.ones((16, CELLS), BF16)
    drop_wide[...] = jnp.zeros_like(drop_wide)
    drop_wide[0:TR] = drop[...].astype(F32)

    def prepare(step, here):
        squash = jax.nn.sigmoid(dot(w_in_t[512:640], stack[0:128, here]))
        lane = lax.broadcasted_iota(jnp.int32, (32, WIDE), 1)
        chosen = ((lane >> 6) & 1) * HALF + (lane >> 7) + 2 * step
        pick = (lax.broadcasted_iota(jnp.int32, (32, WIDE), 0) == chosen).astype(BF16)
        bits = dot_tn(drop_wide[...].astype(BF16), pick)
        kept = bits * (1.0 / KEEP_RATE)
        upstream = turned(grad_cells, step)
        cot_t[:, here] = upstream
        lift_keep[:, here] = kept * squash
        pulled = upstream * kept * squash
        logit_keep[:, here] = pulled * (1.0 - squash)
        lifted_back = pulled.astype(BF16)
        d_lifted[:, here] = lifted_back
        pulled_mixed = dot(w_out[...], lifted_back)
        grad_mixed[:, here] = pulled_mixed
        scaled = pulled_mixed * columns[2]
        centered_mixed[:, here] = scaled - mean0(scaled)

    grad_cells[...] = cot[...].astype(F32)
    each(prepare)
    arrived(got_a, 0)
    assemble(got_a, left)
    for block in range(4):
        here = slice(128 * block, 128 * block + 128)
        left_t[here] = dot_nt(eye[...], left[:, here]).astype(BF16)
    arrived(got_b, 1)
    assemble(got_b, right)
    square[...] = dot(left_t[...], right[...])
    split(square, send_p)
    send(send_p, got_p, 2)

    arrived(got_p, 2)
    flat_a[0:BLOCK] = got_p[...].astype(F32)

    def tail_back(step, here):
        cells = gather(flat_a, step)
        centered = cells - mean0(cells)
        root = lax.rsqrt(mean0(centered * centered) + LN_EPS)
        rough = centered * root
        mid_hat[:, here] = rough
        pulled = centered_mixed[:, here]
        scatter(flat_b, step, root * (pulled - rough * mean0(pulled * rough)))

    each(tail_back)
    send_d[...] = flat_b[0:BLOCK].astype(BF16)
    send(send_d, got_d, 3)

    totals[...] = jnp.zeros_like(totals)

    def total(which, values):
        totals[which] += values[:, :128] + values[:, 128:]

    def tail_front(step, here):
        rough = mid_hat[:, here]
        blended = (rough * columns[2] + columns[3]).astype(BF16)
        mixed[:, here] = blended
        lifted = dot(w_out_t[...], blended)
        turn_back(result_cells, step, (pair_t[:, here] + lift_keep[:, here] * lifted).astype(BF16))
        logit = (logit_keep[:, here] * lifted).astype(BF16)
        d_all[512:640, here] = logit
        pulled = grad_mixed[:, here]
        total(2, pulled * rough)
        total(3, pulled)

    each(tail_front)
    pair[...] = result_cells[...].astype(BF16)
    hand_result = pltpu.make_async_copy(pair, result, local_sem.at[14])
    hand_result.start()
    sums_flat[...] = jnp.zeros_like(sums_flat)

    def put_sums(which, values):
        sums_flat[pl.ds(which, OWNERS, stride=PART), :] = values[:OWNERS]
        sums_flat[pl.ds(which + 6, OWNERS, stride=PART), :] = values[OWNERS:]

    def put_front(first, last):
        outer = dot_nt(stack[...], d_all[128 * first : 128 * last])
        for which in range(first, last):
            here = slice(128 * (which - first), 128 * (which - first) + 128)
            put_sums(which, outer[0:128, here])
            weight = w_all[:, 128 * which : 128 * which + 128].astype(F32)
            totals[0] += outer[128:256, here] * weight
            totals[1] += outer[256:257, here] * weight

    def put_vector(which):
        sums_flat[12 + which : 13 + which] = jnp.sum(totals[which].T, axis=0, keepdims=True)

    put_front(4, 5)
    put_sums(5, dot_nt(mixed[...], d_lifted[...]))
    put_vector(2)
    put_vector(3)

    arrived(got_d, 3)
    assemble(got_d, turn)
    square[...] = dot_nt(right[...], turn[...])
    split(square, send_ga)
    send(send_ga, got_ga, 4)
    square[...] = dot(left[...], turn[...])
    split(square, send_gb)
    send(send_gb, got_gb, 5)

    def front_back(first, flat, keep, slope):
        def run(step, here):
            cells = gather(flat, step)
            d_all[first : first + 128, here] = (cells * keep[:, here]).astype(BF16)
            d_all[first + 128 : first + 256, here] = (cells * slope[:, here]).astype(BF16)

        return run

    arrived(got_ga, 4)
    flat_a[0:BLOCK] = got_ga[...].astype(F32)
    each(front_back(0, flat_a, keep_a, slope_a))
    put_front(0, 2)
    arrived(got_gb, 5)
    flat_b[0:BLOCK] = got_gb[...].astype(F32)
    each(front_back(256, flat_b, keep_b, slope_b))
    put_front(2, 4)
    put_vector(0)
    put_vector(1)
    sums_send[...] = sums_flat[0:SHARES].astype(BF16)

    chip = (row // 2) * COLS + col
    mine = pl.ds(pl.multiple_of(me * PART, PART), PART)
    owned = pl.ds(pl.multiple_of(chip * PART, PART), PART)

    def start_sum(x, y, z):
        home = part_x[x] + part_y[y] + part_z[z]
        owner = (home // 16) * COLS + lax.rem(home, COLS)
        pltpu.make_async_remote_copy(
            src_ref=sums_send.at[pl.ds(pl.multiple_of(owner * PART, PART), PART)],
            dst_ref=sums_got.at[mine],
            send_sem=send_sem.at[6],
            recv_sem=recv_sem.at[6],
            device_id=place(home),
            device_id_type=pl.DeviceIdType.MESH,
        ).start()

    for x, y, z, _ in partners(1):
        start_sum(x, y, z)

    @pl.when(core == 1)
    def _():
        start_sum(0, 0, 0)

    def finish(step, here):
        pulled = dot(w_all[...], d_all[:, here]) * columns[0]
        rough = hat[:, here]
        back = scale[:, here] * (pulled - mean0(pulled) - rough * mean0(pulled * rough))
        turn_back(grad_cells, step, (cot_t[:, here] + back).astype(BF16))

    each(finish)
    cot[...] = grad_cells[...].astype(BF16)
    hand_grad = pltpu.make_async_copy(cot, pair_grad, local_sem.at[15])
    hand_grad.start()

    @pl.when(core == 0)
    def _():
        sums_got[mine] = sums_send[owned]
        arrived(sums_got, 6)
        whole = jnp.sum(sums_got[...].astype(F32).reshape(DEVICES, PART, 128), axis=0)
        share[...] = (whole * (1.0 / TOKENS)).astype(BF16)

        for offset in partners(2):
            pltpu.make_async_remote_copy(
                src_ref=share,
                dst_ref=sums.at[owned],
                send_sem=send_sem.at[7],
                recv_sem=recv_sem.at[7],
                device_id=place(device_at(*offset)),
                device_id_type=pl.DeviceIdType.MESH,
            ).start()

        sums[owned] = share[...]
        settle(sums, recv_sem, 7, (OWNERS - 1) * PART)
        settle(sums_got, send_sem, 7, (DEVICES - 1) * PART)
        settle(sums_send, send_sem, 6, (OWNERS - 1) * PART)

    @pl.when(core == 1)
    def _():
        settle(sums, recv_sem, 7, OWNERS * PART)
        settle(sums_send, send_sem, 6, OWNERS * PART)

    hand_sums = pltpu.make_async_copy(sums, all_sums, local_sem.at[16])
    hand_sums.start()
    for slot, source in enumerate((send_a, send_b, send_p, send_d, send_ga, send_gb)):
        settle(source, send_sem, slot, (DEVICES - 1) * PART)
    for hand in (hand_result, hand_grad, hand_sums):
        hand.wait()


def hand_out(*refs):
    inputs, outputs, refs = refs[:3], refs[3:15], refs[15:]
    held, sums_flat, ready, sem = refs[:3], refs[3], refs[4:14], refs[14]
    fetches = [
        pltpu.make_async_copy(inputs[which], held[which], sem.at[which]) for which in range(3)
    ]
    hands = [
        pltpu.make_async_copy(held[which], outputs[which], sem.at[3 + which]) for which in range(2)
    ]
    hands += [
        pltpu.make_async_copy(ready[which], outputs[2 + which], sem.at[5 + which])
        for which in range(10)
    ]
    for which in (2, 0, 1):
        fetches[which].start()
    fetches[2].wait()
    sums_flat[0:SHARES] = held[2][...].astype(F32)
    for which in range(6):
        ready[which][0:OWNERS] = sums_flat[pl.ds(which, OWNERS, stride=PART), :]
        ready[which][OWNERS:] = sums_flat[pl.ds(which + 6, OWNERS, stride=PART), :]
        hands[2 + which].start()
    for which in range(4):
        ready[6 + which][...] = sums_flat[12 + which : 13 + which]
        hands[8 + which].start()
    for which in range(2):
        fetches[which].wait()
        hands[which].start()
    for hand in hands:
        hand.wait()


def body(pair, cotangent, *rest):
    weights, vectors, drop_bits, tok_mask = rest[:6], rest[6:10], rest[10], rest[11]
    vmem = pltpu.VMEM
    block = vmem((DEVICES * PART, 128), BF16)
    blocks = [block] * 12
    squares = [vmem((SIDE, SIDE), BF16)] * 4 + [vmem((SIDE, SIDE), F32)]
    flats = [vmem((BLOCK + PART, 128), F32)] * 2
    half, full = vmem((128, CELLS), BF16), vmem((128, CELLS), F32)
    square, tile = vmem((128, 128), BF16), (TR * TC, 128)
    scratch = [vmem(tile, BF16)] * 2 + [square] * 6 + [vmem((1, 128), F32)] * 4
    scratch += [vmem((TR, 128), jnp.int32), vmem((1, TOKENS), jnp.int32)]
    scratch += [vmem(tile, F32)] * 2
    scratch += [vmem((2 * TC, 128), BF16), vmem((OWNERS * PART, 128), BF16)]
    scratch += blocks + squares + flats
    scratch += [vmem((128, 128), BF16), vmem((640, 128), BF16), vmem((128, 128), BF16)]
    scratch += [vmem((128, 640), BF16), vmem((4, 128, WIDE), F32), vmem((32, 128), F32)]
    scratch += [vmem((272, CELLS), BF16), full, vmem((1, CELLS), F32)] + [full] * 8
    scratch += [half, full, full, full, half, vmem((640, CELLS), BF16)]
    scratch += [vmem((4, 128, 128), F32), vmem((SHARES + PART, 128), F32)]
    scratch += [vmem((OWNERS * PART, 128), BF16), block, vmem((PART, 128), BF16)]
    scratch += [pltpu.SemaphoreType.DMA((8,))] * 2 + [pltpu.SemaphoreType.DMA((17,))]
    anywhere = pl.BlockSpec(memory_space=pl.ANY)
    done = pl.pallas_call(
        kernel,
        out_shape=[
            jax.ShapeDtypeStruct(tile, BF16),
            jax.ShapeDtypeStruct(tile, BF16),
            jax.ShapeDtypeStruct((OWNERS * PART, 128), BF16),
        ],
        in_specs=[anywhere] * 14,
        out_specs=[anywhere] * 3,
        scratch_shapes=scratch,
        compiler_params=pltpu.CompilerParams(
            collective_id=0, has_side_effects=True, vmem_limit_bytes=60 * 2**20
        ),
    )(
        pair.reshape(tile),
        cotangent.reshape(tile),
        *weights,
        *(vector.reshape(1, 128) for vector in vectors),
        drop_bits,
        tok_mask.reshape(1, TOKENS),
    )
    outs = pl.pallas_call(
        hand_out,
        out_shape=[jax.ShapeDtypeStruct(tile, BF16)] * 2
        + [jax.ShapeDtypeStruct((128, 128), F32)] * 6
        + [jax.ShapeDtypeStruct((1, 128), F32)] * 4,
        in_specs=[anywhere] * 3,
        out_specs=[anywhere] * 12,
        scratch_shapes=[vmem(tile, BF16)] * 2
        + [vmem((SHARES, 128), BF16), vmem((SHARES + PART, 128), F32)]
        + [vmem((128, 128), F32)] * 6
        + [vmem((1, 128), F32)] * 4
        + [pltpu.SemaphoreType.DMA((15,))],
        compiler_params=pltpu.CompilerParams(vmem_limit_bytes=60 * 2**20),
    )(*done)
    result, pair_grad = outs[0].reshape(TR, TC, 128), outs[1].reshape(TR, TC, 128)
    return (result, pair_grad) + tuple(outs[2:8]) + tuple(out.reshape(128) for out in outs[8:])


def solution(mesh):
    tiles = P("row", "col", None)
    return jax.shard_map(
        body,
        mesh=mesh,
        in_specs=(tiles, tiles) + (P(),) * 10 + (P("row", None), P()),
        out_specs=(tiles, tiles) + (P(),) * 10,
        check_vma=False,
    )
```

```python
import jax
import jax.numpy as jnp
from jax import lax
from jax.experimental import pallas as pl
from jax.experimental.pallas import tpu as pltpu
from jax.sharding import PartitionSpec as P

LN_EPS = 1e-05
KEEP_RATE = 0.75
ROWS, COLS = 16, 8
DEVICES = ROWS * COLS
TR, TC = 28, 56
TOKENS = 448
WIDE = 256
STEPS = 7
CELLS = WIDE * STEPS
SIDE = 512
PART = 16
HALF = 14
BLOCK = DEVICES * PART
OWNERS = DEVICES // 2
SHARES = OWNERS * PART
BF16 = jnp.bfloat16
F32 = jnp.float32


def partners(cores):
    offsets = [
        (x, y, z, core)
        for x in range(4)
        for y in range(4)
        for z in range(4)
        for core in range(cores)
        if x or y or z or core
    ]

    def rank(offset):
        far = sum(min(step, 4 - step) for step in offset[:3])
        x, y, z, core = offset
        return -far, (29 * x + 13 * y + 7 * z + 17 * core) % 31, offset

    return sorted(offsets, key=rank)


def dot(left, right):
    return jnp.dot(left, right, preferred_element_type=F32)


def dot_nt(left, right):
    return lax.dot_general(left, right, (((1,), (1,)), ((), ())), preferred_element_type=F32)


def dot_tn(left, right):
    return lax.dot_general(left, right, (((0,), (0,)), ((), ())), preferred_element_type=F32)


def mean0(values):
    return jnp.mean(values, axis=0, keepdims=True)


def swap_halves(first, second):
    low = lax.broadcasted_iota(jnp.int32, first.shape, 1) < 64
    turned_first = pltpu.roll(first, 64, 1)
    turned_second = pltpu.roll(second, 64, 1)
    return jnp.where(low, first, turned_second), jnp.where(low, turned_first, second)


def kernel(*refs):
    inputs, refs = refs[:14], refs[14:]
    outputs, refs = refs[:3], refs[3:]
    run_kernel(inputs, outputs, refs[:14], *refs[14:])


def run_kernel(
    inputs,
    outputs,
    local,
    result_cells,
    grad_cells,
    pick_cells,
    sums,
    send_a,
    send_b,
    send_p,
    send_d,
    send_ga,
    send_gb,
    got_a,
    got_b,
    got_p,
    got_d,
    got_ga,
    got_gb,
    left,
    left_t,
    right,
    turn,
    square,
    flat_a,
    flat_b,
    eye,
    w_in_t,
    w_out_t,
    w_all,
    columns,
    drop_wide,
    stack,
    hat,
    scale,
    keep_a,
    slope_a,
    keep_b,
    slope_b,
    pair_t,
    cot_t,
    lift_keep,
    logit_keep,
    d_lifted,
    grad_mixed,
    centered_mixed,
    mid_hat,
    mixed,
    d_all,
    totals,
    sums_flat,
    sums_send,
    sums_got,
    share,
    send_sem,
    recv_sem,
    local_sem,
):
    result, pair_grad, all_sums = outputs
    pair, cot, w_a_proj, w_a_gate, w_b_proj, w_b_gate, w_gate, w_out = local[:8]
    in_gain, in_bias, mid_gain, mid_bias, drop, tok = local[8:]
    fetches = [
        pltpu.make_async_copy(inputs[which], local[which], local_sem.at[which])
        for which in range(14)
    ]
    for fetch in fetches:
        fetch.start()
    row, col = lax.axis_index("row"), lax.axis_index("col")
    me = row * COLS + col
    barrier = pltpu.get_barrier_semaphore()

    core = lax.rem(row, 2)
    at_x, at_y, at_z = lax.rem(row // 2, 2) * 2 + col // 4, row // 4, lax.rem(col, 4)
    steps_x = [lax.rem(at_x + step, 4) for step in range(4)]
    row_x = [(step // 2) * 2 for step in steps_x]
    row_y = [lax.rem(at_y + step, 4) * 4 for step in range(4)]
    row_core = [core, 1 - core]
    col_x = [lax.rem(step, 2) * 4 for step in steps_x]
    col_z = [lax.rem(at_z + step, 4) for step in range(4)]

    def device_at(x, y, z, other_core):
        return row_y[y] + row_x[x] + row_core[other_core], col_x[x] + col_z[z]

    for offset in partners(2):
        pl.semaphore_signal(
            barrier,
            inc=1,
            device_id=device_at(*offset),
            device_id_type=pl.DeviceIdType.MESH,
        )

    def send(source, target, slot, size=PART):
        mine = pl.ds(pl.multiple_of(me * size, size), size)

        for offset in partners(2):
            there = device_at(*offset)
            peer = there[0] * COLS + there[1]
            pltpu.make_async_remote_copy(
                src_ref=source.at[pl.ds(pl.multiple_of(peer * size, size), size)],
                dst_ref=target.at[mine],
                send_sem=send_sem.at[slot],
                recv_sem=recv_sem.at[slot],
                device_id=there,
                device_id_type=pl.DeviceIdType.MESH,
            ).start()
        target[mine] = source[mine]

    def settle(ref, sem, slot, length):
        some = ref.at[pl.ds(0, length)]
        pltpu.make_async_copy(some, some, sem.at[slot]).wait()

    def arrived(target, slot, size=PART):
        settle(target, recv_sem, slot, (DEVICES - 1) * size)

    def lanes(step):
        return pl.ds(pl.multiple_of(step * WIDE, WIDE), WIDE)

    def each(body):
        def run(step, carry):
            body(step, lanes(step))
            return carry

        lax.fori_loop(0, STEPS, run, 0, unroll=STEPS)

    def scatter(flat, step, values, stride=PART, shift=0):
        flat[pl.ds(2 * step + shift, 128, stride=stride), :] = values[:, :128]
        flat[pl.ds(2 * step + shift + 1, 128, stride=stride), :] = values[:, 128:]

    def gather(flat, step):
        return jnp.concatenate(
            [
                flat[pl.ds(2 * step, 128, stride=PART), :],
                flat[pl.ds(2 * step + 1, 128, stride=PART), :],
            ],
            axis=1,
        )

    def tile_rows(step, part):
        first = pl.multiple_of((2 * step + part) * TC, 8)
        second = pl.multiple_of((2 * step + part + HALF) * TC, 8)
        return pl.ds(first, TC), pl.ds(second, TC)

    def turned(ref, step):
        parts = []
        for part in range(2):
            first, second = tile_rows(step, part)
            cells = jnp.concatenate([ref[first], ref[second]], axis=0).astype(BF16)
            parts.append(dot_tn(cells, pick_cells[...]))
        return jnp.concatenate(parts, axis=1)

    def turn_back(ref, step, values):
        for part in range(2):
            first, second = tile_rows(step, part)
            cells = dot_nt(pick_cells[...], values[:, 128 * part : 128 * part + 128])
            ref[first] = cells[:TC]
            ref[second] = cells[TC:]

    def assemble(blocks, matrix, stride=PART, shift=0):
        def run(index, carry):
            base = pl.multiple_of(index * COLS * stride, COLS * stride)
            top = pl.multiple_of(index * 32, 32)
            for pick in range(4):
                one = blocks[pl.ds(base + 2 * pick * stride + shift, PART)].astype(F32)
                two = blocks[pl.ds(base + (2 * pick + 1) * stride + shift, PART)].astype(F32)
                upper, lower = swap_halves(one, two)
                here = pl.ds(128 * pick, 128)
                matrix[pl.ds(top, PART), here] = upper.astype(BF16)
                matrix[pl.ds(top + PART, PART), here] = lower.astype(BF16)
            return carry

        lax.fori_loop(0, ROWS, run, 0, unroll=ROWS)

    def split(matrix, blocks):
        def run(index, carry):
            base = pl.multiple_of(index * 128, 128)
            top = pl.multiple_of(index * 32, 32)
            for pick in range(4):
                here = pl.ds(128 * pick, 128)
                upper = matrix[pl.ds(top, PART), here]
                lower = matrix[pl.ds(top + PART, PART), here]
                one, two = swap_halves(upper, lower)
                blocks[pl.ds(base + 32 * pick, PART)] = one.astype(BF16)
                blocks[pl.ds(base + 32 * pick + PART, PART)] = two.astype(BF16)
            return carry

        lax.fori_loop(0, ROWS, run, 0, unroll=ROWS)

    for spare in range(HALF, PART):
        flat_a[pl.ds(spare, 128, stride=PART), :] = jnp.zeros((128, 128), F32)
        flat_b[pl.ds(spare, 128, stride=PART), :] = jnp.zeros((128, 128), F32)
    eye[...] = (
        lax.broadcasted_iota(jnp.int32, (128, 128), 0)
        == lax.broadcasted_iota(jnp.int32, (128, 128), 1)
    ).astype(BF16)
    lane = lax.broadcasted_iota(jnp.int32, (2 * TC, 128), 1)
    wanted = (lane >> 6) * TC + ((lane >> 4) & 3) * HALF + (lane & 15)
    chosen_cell = lax.broadcasted_iota(jnp.int32, (2 * TC, 128), 0) == wanted
    chosen_cell = jnp.where(chosen_cell, 1.0, 0.0) * jnp.where((lane & 15) < HALF, 1.0, 0.0)
    pick_cells[...] = chosen_cell.astype(BF16)
    for fetch in fetches:
        fetch.wait()
    def put_weight(which, weight):
        here = slice(128 * which, 128 * which + 128)
        w_in_t[here] = dot_nt(eye[...], weight[...]).astype(BF16)
        w_all[:, here] = weight[...]

    def put_column(which, vector):
        column = jnp.broadcast_to(vector[...], (128, 128)).T
        columns[which] = jnp.concatenate([column, column], axis=1)

    put_weight(0, w_a_proj)
    put_weight(1, w_a_gate)
    put_column(0, in_gain)
    put_column(1, in_bias)
    live = jnp.sum(tok[...].astype(F32), axis=1, keepdims=True)

    def cell_mask(step):
        lane = lax.broadcasted_iota(jnp.int32, (1, WIDE), 1)
        tile_row = ((lane >> 6) & 1) * HALF + (lane >> 7) + 2 * step
        within = lane & 15
        tile_col = ((lane >> 4) & 3) * HALF + within
        grid_row = (tile_row + row * TR).astype(F32)
        grid_col = (tile_col + col * TC).astype(F32)
        one = jnp.where(grid_row < live, 1.0, 0.0) * jnp.where(grid_col < live, 1.0, 0.0)
        return one * jnp.where(within < HALF, 1.0, 0.0)

    def front(step, here, weights, keep, slope, flat):
        logits = dot(w_in_t[weights], stack[0:128, here])
        squash = jax.nn.sigmoid(logits[128:])
        masked = squash * cell_mask(step)
        values = logits[:128] * masked
        keep[:, here] = masked
        slope[:, here] = values * (1.0 - squash)
        scatter(flat, step, values)

    def front_a(step, here):
        cells = turned(result_cells, step)
        pair_t[:, here] = cells
        centered = cells - mean0(cells)
        root = lax.rsqrt(mean0(centered * centered) + LN_EPS)
        rough = centered * root
        hat[:, here] = rough
        scale[:, here] = root
        stack[0:128, here] = (rough * columns[0] + columns[1]).astype(BF16)
        stack[128:256, here] = rough.astype(BF16)
        front(step, here, slice(0, 256), keep_a, slope_a, flat_a)

    result_cells[...] = pair[...].astype(F32)
    each(front_a)
    send_a[...] = flat_a[0:BLOCK].astype(BF16)
    pl.semaphore_wait(barrier, DEVICES - 1)
    send(send_a, got_a, 0)
    put_weight(2, w_b_proj)
    put_weight(3, w_b_gate)
    each(lambda step, here: front(step, here, slice(256, 512), keep_b, slope_b, flat_b))
    send_b[...] = flat_b[0:BLOCK].astype(BF16)
    send(send_b, got_b, 1)
    put_weight(4, w_gate)
    w_out_t[...] = dot_nt(eye[...], w_out[...]).astype(BF16)
    put_column(2, mid_gain)
    put_column(3, mid_bias)
    stack[256:272] = jnp.ones((16, CELLS), BF16)
    drop_wide[...] = jnp.zeros_like(drop_wide)
    drop_wide[0:TR] = drop[...].astype(F32)

    def prepare(step, here):
        squash = jax.nn.sigmoid(dot(w_in_t[512:640], stack[0:128, here]))
        lane = lax.broadcasted_iota(jnp.int32, (32, WIDE), 1)
        chosen = ((lane >> 6) & 1) * HALF + (lane >> 7) + 2 * step
        pick = (lax.broadcasted_iota(jnp.int32, (32, WIDE), 0) == chosen).astype(BF16)
        bits = dot_tn(drop_wide[...].astype(BF16), pick)
        kept = bits * (1.0 / KEEP_RATE)
        upstream = turned(grad_cells, step)
        cot_t[:, here] = upstream
        lift_keep[:, here] = kept * squash
        pulled = upstream * kept * squash
        logit_keep[:, here] = pulled * (1.0 - squash)
        lifted_back = pulled.astype(BF16)
        d_lifted[:, here] = lifted_back
        pulled_mixed = dot(w_out[...], lifted_back)
        grad_mixed[:, here] = pulled_mixed
        scaled = pulled_mixed * columns[2]
        centered_mixed[:, here] = scaled - mean0(scaled)

    grad_cells[...] = cot[...].astype(F32)
    each(prepare)
    arrived(got_a, 0)
    assemble(got_a, left)
    for block in range(4):
        here = slice(128 * block, 128 * block + 128)
        left_t[here] = dot_nt(eye[...], left[:, here]).astype(BF16)
    arrived(got_b, 1)
    assemble(got_b, right)
    square[...] = dot(left_t[...], right[...])
    split(square, send_p)
    send(send_p, got_p, 2)

    arrived(got_p, 2)
    flat_a[0:BLOCK] = got_p[...].astype(F32)

    def tail_back(step, here):
        cells = gather(flat_a, step)
        centered = cells - mean0(cells)
        root = lax.rsqrt(mean0(centered * centered) + LN_EPS)
        rough = centered * root
        mid_hat[:, here] = rough
        pulled = centered_mixed[:, here]
        scatter(flat_b, step, root * (pulled - rough * mean0(pulled * rough)))

    each(tail_back)
    send_d[...] = flat_b[0:BLOCK].astype(BF16)
    send(send_d, got_d, 3)

    totals[...] = jnp.zeros_like(totals)

    def total(which, values):
        totals[which] += values[:, :128] + values[:, 128:]

    def tail_front(step, here):
        rough = mid_hat[:, here]
        blended = (rough * columns[2] + columns[3]).astype(BF16)
        mixed[:, here] = blended
        lifted = dot(w_out_t[...], blended)
        turn_back(result_cells, step, (pair_t[:, here] + lift_keep[:, here] * lifted).astype(BF16))
        logit = (logit_keep[:, here] * lifted).astype(BF16)
        d_all[512:640, here] = logit
        pulled = grad_mixed[:, here]
        total(2, pulled * rough)
        total(3, pulled)

    each(tail_front)
    pair[...] = result_cells[...].astype(BF16)
    hand_result = pltpu.make_async_copy(pair, result, local_sem.at[14])
    hand_result.start()
    sums_flat[...] = jnp.zeros_like(sums_flat)

    def put_sums(which, values):
        sums_flat[pl.ds(which, OWNERS, stride=PART), :] = values[:OWNERS]
        sums_flat[pl.ds(which + 6, OWNERS, stride=PART), :] = values[OWNERS:]

    def put_front(first, last):
        outer = dot_nt(stack[...], d_all[128 * first : 128 * last])
        for which in range(first, last):
            here = slice(128 * (which - first), 128 * (which - first) + 128)
            put_sums(which, outer[0:128, here])
            weight = w_all[:, 128 * which : 128 * which + 128].astype(F32)
            totals[0] += outer[128:256, here] * weight
            totals[1] += outer[256:257, here] * weight

    def put_vector(which):
        sums_flat[12 + which : 13 + which] = jnp.sum(totals[which].T, axis=0, keepdims=True)

    put_front(4, 5)
    put_sums(5, dot_nt(mixed[...], d_lifted[...]))
    put_vector(2)
    put_vector(3)

    arrived(got_d, 3)
    assemble(got_d, turn)
    square[...] = dot_nt(right[...], turn[...])
    split(square, send_ga)
    send(send_ga, got_ga, 4)
    square[...] = dot(left[...], turn[...])
    split(square, send_gb)
    send(send_gb, got_gb, 5)

    def front_back(first, flat, keep, slope):
        def run(step, here):
            cells = gather(flat, step)
            d_all[first : first + 128, here] = (cells * keep[:, here]).astype(BF16)
            d_all[first + 128 : first + 256, here] = (cells * slope[:, here]).astype(BF16)

        return run

    arrived(got_ga, 4)
    flat_a[0:BLOCK] = got_ga[...].astype(F32)
    each(front_back(0, flat_a, keep_a, slope_a))
    put_front(0, 2)
    arrived(got_gb, 5)
    flat_b[0:BLOCK] = got_gb[...].astype(F32)
    each(front_back(256, flat_b, keep_b, slope_b))
    put_front(2, 4)
    put_vector(0)
    put_vector(1)
    sums_send[...] = sums_flat[0:SHARES].astype(BF16)

    chip = (row // 2) * COLS + col
    mine = pl.ds(pl.multiple_of(me * PART, PART), PART)
    owned = pl.ds(pl.multiple_of(chip * PART, PART), PART)

    def start_sum(x, y, z):
        there = row_y[y] + row_x[x], col_x[x] + col_z[z]
        owner = there[0] * (COLS // 2) + there[1]
        pltpu.make_async_remote_copy(
            src_ref=sums_send.at[pl.ds(pl.multiple_of(owner * PART, PART), PART)],
            dst_ref=sums_got.at[mine],
            send_sem=send_sem.at[6],
            recv_sem=recv_sem.at[6],
            device_id=there,
            device_id_type=pl.DeviceIdType.MESH,
        ).start()

    for x, y, z, _ in partners(1):
        start_sum(x, y, z)

    @pl.when(core == 1)
    def _():
        start_sum(0, 0, 0)

    def finish(step, here):
        pulled = dot(w_all[...], d_all[:, here]) * columns[0]
        rough = hat[:, here]
        back = scale[:, here] * (pulled - mean0(pulled) - rough * mean0(pulled * rough))
        turn_back(grad_cells, step, (cot_t[:, here] + back).astype(BF16))

    each(finish)
    cot[...] = grad_cells[...].astype(BF16)
    hand_grad = pltpu.make_async_copy(cot, pair_grad, local_sem.at[15])
    hand_grad.start()

    @pl.when(core == 0)
    def _():
        sums_got[mine] = sums_send[owned]
        arrived(sums_got, 6)
        whole = jnp.sum(sums_got[...].astype(F32).reshape(DEVICES, PART, 128), axis=0)
        share[...] = (whole * (1.0 / TOKENS)).astype(BF16)

        for offset in partners(2):
            pltpu.make_async_remote_copy(
                src_ref=share,
                dst_ref=sums.at[owned],
                send_sem=send_sem.at[7],
                recv_sem=recv_sem.at[7],
                device_id=device_at(*offset),
                device_id_type=pl.DeviceIdType.MESH,
            ).start()

        sums[owned] = share[...]
        settle(sums, recv_sem, 7, (OWNERS - 1) * PART)
        settle(sums_got, send_sem, 7, (DEVICES - 1) * PART)
        settle(sums_send, send_sem, 6, (OWNERS - 1) * PART)

    @pl.when(core == 1)
    def _():
        settle(sums, recv_sem, 7, OWNERS * PART)
        settle(sums_send, send_sem, 6, OWNERS * PART)

    hand_sums = pltpu.make_async_copy(sums, all_sums, local_sem.at[16])
    hand_sums.start()
    for slot, source in enumerate((send_a, send_b, send_p, send_d, send_ga, send_gb)):
        settle(source, send_sem, slot, (DEVICES - 1) * PART)
    for hand in (hand_result, hand_grad, hand_sums):
        hand.wait()


def hand_out(*refs):
    inputs, outputs, refs = refs[:3], refs[3:15], refs[15:]
    held, sums_flat, ready, sem = refs[:3], refs[3], refs[4:14], refs[14]
    fetches = [
        pltpu.make_async_copy(inputs[which], held[which], sem.at[which]) for which in range(3)
    ]
    hands = [
        pltpu.make_async_copy(held[which], outputs[which], sem.at[3 + which]) for which in range(2)
    ]
    hands += [
        pltpu.make_async_copy(ready[which], outputs[2 + which], sem.at[5 + which])
        for which in range(10)
    ]
    for which in (2, 0, 1):
        fetches[which].start()
    fetches[2].wait()
    sums_flat[0:SHARES] = held[2][...].astype(F32)
    for which in range(6):
        ready[which][0:OWNERS] = sums_flat[pl.ds(which, OWNERS, stride=PART), :]
        ready[which][OWNERS:] = sums_flat[pl.ds(which + 6, OWNERS, stride=PART), :]
        hands[2 + which].start()
    for which in range(4):
        ready[6 + which][...] = sums_flat[12 + which : 13 + which]
        hands[8 + which].start()
    for which in range(2):
        fetches[which].wait()
        hands[which].start()
    for hand in hands:
        hand.wait()


def body(pair, cotangent, *rest):
    weights, vectors, drop_bits, tok_mask = rest[:6], rest[6:10], rest[10], rest[11]
    vmem = pltpu.VMEM
    block = vmem((DEVICES * PART, 128), BF16)
    blocks = [block] * 12
    squares = [vmem((SIDE, SIDE), BF16)] * 4 + [vmem((SIDE, SIDE), F32)]
    flats = [vmem((BLOCK + PART, 128), F32)] * 2
    half, full = vmem((128, CELLS), BF16), vmem((128, CELLS), F32)
    square, tile = vmem((128, 128), BF16), (TR * TC, 128)
    scratch = [vmem(tile, BF16)] * 2 + [square] * 6 + [vmem((1, 128), F32)] * 4
    scratch += [vmem((TR, 128), jnp.int32), vmem((1, TOKENS), jnp.int32)]
    scratch += [vmem(tile, F32)] * 2
    scratch += [vmem((2 * TC, 128), BF16), vmem((OWNERS * PART, 128), BF16)]
    scratch += blocks + squares + flats
    scratch += [vmem((128, 128), BF16), vmem((640, 128), BF16), vmem((128, 128), BF16)]
    scratch += [vmem((128, 640), BF16), vmem((4, 128, WIDE), F32), vmem((32, 128), F32)]
    scratch += [vmem((272, CELLS), BF16), full, vmem((1, CELLS), F32)] + [full] * 8
    scratch += [half, full, full, full, half, vmem((640, CELLS), BF16)]
    scratch += [vmem((4, 128, 128), F32), vmem((SHARES + PART, 128), F32)]
    scratch += [vmem((OWNERS * PART, 128), BF16), block, vmem((PART, 128), BF16)]
    scratch += [pltpu.SemaphoreType.DMA((8,))] * 2 + [pltpu.SemaphoreType.DMA((17,))]
    anywhere = pl.BlockSpec(memory_space=pl.ANY)
    done = pl.pallas_call(
        kernel,
        out_shape=[
            jax.ShapeDtypeStruct(tile, BF16),
            jax.ShapeDtypeStruct(tile, BF16),
            jax.ShapeDtypeStruct((OWNERS * PART, 128), BF16),
        ],
        in_specs=[anywhere] * 14,
        out_specs=[anywhere] * 3,
        scratch_shapes=scratch,
        compiler_params=pltpu.CompilerParams(
            collective_id=0, has_side_effects=True, vmem_limit_bytes=60 * 2**20
        ),
    )(
        pair.reshape(tile),
        cotangent.reshape(tile),
        *weights,
        *(vector.reshape(1, 128) for vector in vectors),
        drop_bits,
        tok_mask.reshape(1, TOKENS),
    )
    outs = pl.pallas_call(
        hand_out,
        out_shape=[jax.ShapeDtypeStruct(tile, BF16)] * 2
        + [jax.ShapeDtypeStruct((128, 128), F32)] * 6
        + [jax.ShapeDtypeStruct((1, 128), F32)] * 4,
        in_specs=[anywhere] * 3,
        out_specs=[anywhere] * 12,
        scratch_shapes=[vmem(tile, BF16)] * 2
        + [vmem((SHARES, 128), BF16), vmem((SHARES + PART, 128), F32)]
        + [vmem((128, 128), F32)] * 6
        + [vmem((1, 128), F32)] * 4
        + [pltpu.SemaphoreType.DMA((15,))],
        compiler_params=pltpu.CompilerParams(vmem_limit_bytes=60 * 2**20),
    )(*done)
    result, pair_grad = outs[0].reshape(TR, TC, 128), outs[1].reshape(TR, TC, 128)
    return (result, pair_grad) + tuple(outs[2:8]) + tuple(out.reshape(128) for out in outs[8:])


def solution(mesh):
    tiles = P("row", "col", None)
    return jax.shard_map(
        body,
        mesh=mesh,
        in_specs=(tiles, tiles) + (P(),) * 10 + (P("row", None), P()),
        out_specs=(tiles, tiles) + (P(),) * 10,
        check_vma=False,
    )
```
